256 devices in a mesh: dp: 32 (over y, z_hi, core), seq: 8 (over x, z_lo).
Axes of the slice: x: 4, y: 4, z: 8 (z_hi: 4, z_lo: 2; z = z_hi * 2 + z_lo), core: 2. Of those that a mesh axis runs over, the one named last changes fastest.
Arguments:
- tokens: bfloat16 [32, 8192, 768], P('dp', 'seq'), may hold values from -6 to 6
- depthwise_weight: float32 [3, 768], replicated, may hold values from -4 to 4
- down_weight: bfloat16 [1536, 1536], replicated, may hold values from -0.15625 to 0.15625
- bott_dw: float32 [3, 1536], replicated, may hold values from -4 to 4
- bott_weight: bfloat16 [1536, 768], replicated, may hold values from -0.15625 to 0.15625
- cotangent: bfloat16 [32, 4096, 768], P('dp', 'seq'), may hold values from -6 to 6
- plan_owner: int32 [32, 256], P('dp'), may hold values from 0 to 7, as said below
- plan_slot: int32 [32, 256], P('dp'), may hold values from 0 to 3, as said below
- counts: int32 [32, 8], P('dp'), may hold values from 8 to 32, as said below
Outputs:
- owned_panels: bfloat16 [32, 256, 16, 1536], P('dp', 'seq')
- bottleneck: bfloat16 [32, 4096, 768], P('dp', 'seq')
- grad_bott: float32 [1536, 768], P(('dp', 'seq'))
The draws below stay inside these ranges and needn't reach their ends.
Inputs may be any that keep to these rules, and one draw needn't show every extreme that they name: `plan_owner`: for each window and each source device s, the 32 groups of s fill each owner's 4 slots 0 to 3 for s exactly once: no two groups of s share an owner and slot. `plan_slot`: slot of a group among the groups its source sends to its owner. `counts`: in every window some device has all 32 groups mappable.
All inputs are finite; a program needn't handle non-finite values.
Results may differ from the reference program's by a relative error of at most 0.013.
Values may be sent and summed in bfloat16 or wider, within the bound.
A program may use at most 128 MiB of HBM per device.

```python
import jax
import jax.numpy as jnp
from jax import lax

C = 768
C2 = 1536
DILATION_STEP = 8
GROUPS_DEV = 32
WINDOWS = 32
WINDOW_LENGTH = 8192
HALF = 16
HLEN = 4096
GROUPS = 256
CAP = 4
N_SEQ = 8


def plan_parts(key):
    base = jax.random.fold_in(key, 11)
    keys = jax.random.split(base, WINDOWS * N_SEQ)
    orders = jax.vmap(lambda k: jax.random.permutation(k, GROUPS_DEV))(keys).reshape(WINDOWS, N_SEQ, GROUPS_DEV).astype(jnp.int32)
    shifts = jax.random.randint(jax.random.fold_in(base, 1), (WINDOWS, N_SEQ, 1), 0, N_SEQ).astype(jnp.int32)
    source = jnp.arange(N_SEQ, dtype=jnp.int32)[None, :, None]
    per_pair = GROUPS_DEV // N_SEQ
    owner = (source + shifts + orders // per_pair) % N_SEQ
    slot = orders % per_pair
    return (owner.reshape(WINDOWS, GROUPS).astype(jnp.int32), slot.reshape(WINDOWS, GROUPS).astype(jnp.int32))


def draw_plan_owner(key, part):
    return plan_parts(key)[0]


def draw_plan_slot(key, part):
    return plan_parts(key)[1]


def draw_counts(key, part):
    key = jax.random.fold_in(key, 5)
    drawn = jax.random.randint(jax.random.fold_in(key, 1), (WINDOWS, N_SEQ), GROUPS_DEV // 4, GROUPS_DEV + 1).astype(jnp.int32)
    full_one = jax.random.randint(jax.random.fold_in(key, 2), (WINDOWS, 1), 0, N_SEQ).astype(jnp.int32)
    column = jnp.arange(N_SEQ, dtype=jnp.int32)[None, :]
    return jnp.where(column == full_one, GROUPS_DEV, drawn).astype(jnp.int32)


def steps_of(own_key, shape, cuts, least, top_value):
    factor_of, own = 1.0, jax.random.fold_in(own_key, 6)
    for axis_at, parts in cuts:
        draws = jnp.exp(jax.random.uniform(jax.random.fold_in(own, axis_at), (parts,), jnp.float32, least / len(cuts), top_value / len(cuts)))
        factor_of = factor_of * jnp.repeat(draws, shape[axis_at] // parts).reshape([-1 if axis == axis_at else 1 for axis in range(len(shape))])
    return factor_of


def noise(own_key, dims, scale, reach, cuts=(), held_as=jnp.bfloat16):
    values = jax.random.normal(own_key, dims, jnp.float32) * scale
    if len(cuts) > 0:
        values = steps_of(own_key, dims, cuts, -0.22, 0.18) * values
    return jnp.clip(values, min=-reach, max=reach).astype(held_as)


def setup_inputs(seed: int = 0) -> dict:
    seeds = jax.random.split(jax.random.key(seed), 10)
    tokens = noise(seeds[0], (WINDOWS, WINDOW_LENGTH, C), 1.0, 6.0, ((0, 32), (1, 8)))
    depthwise_weight = noise(seeds[1], (3, C), 0.7, 4.0, (), jnp.float32)
    down_weight = noise(seeds[2], (2 * C, C2), (2 * C) ** -0.5, 0.15625)
    bott_dw = noise(seeds[3], (3, C2), 0.7, 4.0, (), jnp.float32)
    bott_weight = noise(seeds[4], (C2, C), C2 ** -0.5, 0.15625)
    cotangent = noise(seeds[5], (WINDOWS, HLEN, C), 1.0, 6.0, ((0, 32), (1, 8)))
    plan_owner = draw_plan_owner(jax.random.fold_in(seeds[9], 71), 0)
    plan_slot = draw_plan_slot(jax.random.fold_in(seeds[9], 71), 0)
    counts = draw_counts(jax.random.fold_in(seeds[9], 71), 0)
    return {"tokens": tokens, "depthwise_weight": depthwise_weight, "down_weight": down_weight, "bott_dw": bott_dw, "bott_weight": bott_weight, "cotangent": cotangent, "plan_owner": plan_owner, "plan_slot": plan_slot, "counts": counts}


def one_window(tokens_w, owner_w, slot_w, counts_w, cot_w, depthwise_weight, down_weight, bott_dw, bott_weight):
    input_float = tokens_w.astype(jnp.float32)
    padded_input = jnp.pad(input_float, ((DILATION_STEP, DILATION_STEP), (0, 0)))
    conv_result = depthwise_weight[0] * padded_input[0:WINDOW_LENGTH] + depthwise_weight[1] * padded_input[DILATION_STEP:DILATION_STEP + WINDOW_LENGTH] + depthwise_weight[2] * padded_input[2 * DILATION_STEP:2 * DILATION_STEP + WINDOW_LENGTH]
    act = (input_float + jax.nn.gelu(conv_result)).astype(jnp.bfloat16)
    pairs = act.reshape(GROUPS * HALF, 2 * C)
    proj = jax.nn.gelu(jnp.dot(pairs, down_weight, preferred_element_type=jnp.float32)).reshape(GROUPS, HALF, C2)
    group_ids = jnp.arange(GROUPS, dtype=jnp.int32)
    source = group_ids // GROUPS_DEV
    mappable = group_ids % GROUPS_DEV < jnp.repeat(counts_w, GROUPS_DEV)
    panel = jnp.where(mappable[:, None, None], proj, 0.0).astype(jnp.bfloat16)
    places = owner_w * GROUPS_DEV + source * CAP + slot_w
    owned = jnp.zeros((GROUPS, HALF, C2), jnp.bfloat16).at[places].set(panel)
    qf = panel.reshape(HLEN, C2).astype(jnp.float32)
    qp = jnp.pad(qf, ((1, 1), (0, 0)))
    mixed = (bott_dw[0] * qp[0:HLEN] + bott_dw[1] * qp[1:HLEN + 1] + bott_dw[2] * qp[2:HLEN + 2]).astype(jnp.bfloat16)
    pre = jnp.dot(mixed, bott_weight, preferred_element_type=jnp.float32)
    out, pullback = jax.vjp(jax.nn.gelu, pre)
    delta = pullback(cot_w.astype(jnp.float32))[0].astype(jnp.bfloat16)
    term = lax.dot_general(mixed, delta, (((0,), (0,)), ((), ())), preferred_element_type=jnp.float32)
    return (owned, out.astype(jnp.bfloat16), term)

def reference(tokens, depthwise_weight, down_weight, bott_dw, bott_weight, cotangent, plan_owner, plan_slot, counts):

    def step(total, items):
        owned, out, term = one_window(items[0], items[1], items[2], items[3], items[4], depthwise_weight, down_weight, bott_dw, bott_weight)
        return (total + term, (owned, out))
    start = jnp.zeros((C2, C), jnp.float32)
    total, (owned_all, out_all) = lax.scan(step, start, (tokens, plan_owner, plan_slot, counts, cotangent))
    return (owned_all, out_all, total)
```

```python
import jax
import jax.numpy as jnp
from jax import lax
from jax.experimental import pallas as pl
from jax.experimental.pallas import tpu as pltpu
from jax.sharding import PartitionSpec as P

C = 768
C2 = 1536
GROUP = 32
GROUPS_DEV = 32
HALF = 16
CAP = 4
N_SEQ = 8
ROWS = 1024
HROWS = 512
PAD = 16
NC = 3
CW = C // NC
MESH = pl.DeviceIdType.MESH
K0 = 0.7978845608028654
K1 = 0.044715
ORDER = (((2, 1), (2, 0)), ((1, 1), (3, 1)), ((1, 0), (3, 0)), ((0, 1), (0, 0)))


def gelu(x):
    return 0.5 * x * (1.0 + jnp.tanh(K0 * (x + K1 * (x * x * x))))


def gelu_both(x):
    square = x * x
    t = jnp.tanh(K0 * x * (1.0 + K1 * square))
    half = 0.5 * (1.0 + t)
    slope = half + 0.5 * x * (1.0 - t * t) * (K0 * (1.0 + 3.0 * K1 * square))
    return x * half, slope


def one_if(n):
    return jnp.clip(n, 0, 1).astype(jnp.float32)


def kernel(
    owner_ref, slot_ref, counts_ref, tokens_ref, dw_ref, down_ref, bdw_ref, bott_ref, cot_ref,
    owned_ref, out_ref, grad_ref,
    place_s, inv_s, tok, down, bott, cot, act_s, outgoing, qf, mixed, mixed_t, result,
    gbuf, csend, crecv, yacc, ysend, yrecv, zacc, zsend, zrecv, ssend, srecv,
    in_sem, halo_send, halo_recv, a_send, a_recv, own_sem, out_sem,
    c_send, c_recv, y_send, y_recv, z_send, z_recv, s_send, s_recv,
):
    dp = lax.axis_index("dp")
    me = lax.axis_index("seq")
    mx, mz = me // 2, me % 2
    core = dp % 2
    zh = (dp // 2) % 4
    my = dp // 8

    def seq_at(kx, kz):
        return ((mx + kx) % 4) * 2 + (mz + kz) % 2

    def dp_of(y, z, c):
        return y * 8 + z * 2 + c

    loads = [
        pltpu.make_async_copy(tokens_ref, tok.at[pl.ds(1, 64)], in_sem.at[0]),
        pltpu.make_async_copy(down_ref, down, in_sem.at[1]),
        pltpu.make_async_copy(bott_ref, bott, in_sem.at[2]),
        pltpu.make_async_copy(cot_ref.at[0], cot, in_sem.at[3]),
    ]
    for load in loads:
        load.start()

    barrier = pltpu.get_barrier_semaphore()
    peers = [(dp, seq_at(k // 2, k % 2)) for k in range(1, 8)]
    peers += [(dp_of(my, zh, 1 - core), me)]
    peers += [(dp_of((my + k) % 4, zh, core), me) for k in range(1, 4)]
    peers += [(dp_of(my, (zh + k) % 4, core), me) for k in range(1, 4)]
    for peer in peers:
        pl.semaphore_signal(barrier, inc=1, device_id=peer, device_id_type=MESH)

    def set_place(j, carry):
        place_s[j] = owner_ref[0, me * GROUPS_DEV + j] * CAP + slot_ref[0, me * GROUPS_DEV + j]
        return carry

    lax.fori_loop(0, GROUPS_DEV, set_place, 0)

    def set_inv(p, carry):
        found = jnp.int32(0)
        for j in range(GROUPS_DEV):
            found = found + j * (1 - jnp.minimum(jnp.abs(place_s[j] - p), 1))
        inv_s[p] = jnp.minimum(found, GROUPS_DEV - 1)
        return carry

    lax.fori_loop(0, GROUPS_DEV, set_inv, 0)
    ssend[...] = jnp.zeros_like(ssend)
    pl.semaphore_wait(barrier, len(peers))

    up, dn = (me + 1) % N_SEQ, (me + N_SEQ - 1) % N_SEQ
    halos = [
        pltpu.make_async_remote_copy(
            tokens_ref.at[63], tok.at[0],
            halo_send.at[0], halo_recv.at[0], device_id=(dp, up), device_id_type=MESH),
        pltpu.make_async_remote_copy(
            tokens_ref.at[0], tok.at[65],
            halo_send.at[1], halo_recv.at[1], device_id=(dp, dn), device_id_type=MESH),
    ]
    for h in halos:
        h.start()
    loads[0].wait()
    for h in halos:
        h.wait_recv()

    @pl.when(me == 0)
    def _():
        tok[0] = jnp.zeros((PAD, C), jnp.bfloat16)

    @pl.when(me == N_SEQ - 1)
    def _():
        tok[65] = jnp.zeros((PAD, C), jnp.bfloat16)

    w0, w1, w2 = dw_ref[0:1, :], dw_ref[1:2, :], dw_ref[2:3, :]
    my_count = counts_ref[0, me]

    def act_of(before, here, after):
        return here + gelu(w0 * before + w1 * here + w2 * after)

    def put_act(at, value):
        for b in range(6):
            act_s[b, pl.ds(at, value.shape[0]), :] = value[:, b * 128:b * 128 + 128]

    sends = []
    for step, pair in enumerate(ORDER):
        dests = [seq_at(*offset) for offset in pair]
        for n, dest in enumerate(dests):
            def one_group(slot, carry, n=n, dest=dest):
                group = inv_s[dest * CAP + slot]
                rows = tok[pl.ds(2 * group, 4)].reshape(2 * GROUP, C).astype(jnp.float32)
                put_act((n * CAP + slot) * GROUP, act_of(rows[8:40], rows[16:48], rows[24:56]))
                return carry

            lax.fori_loop(0, CAP, one_group, 0)
        last = step == len(ORDER) - 1
        if last:
            low = tok[0:2].reshape(GROUP, C).astype(jnp.float32)
            high = tok[64:66].reshape(GROUP, C).astype(jnp.float32)
            put_act(256, act_of(low[0:8], low[8:16], low[16:24]))
            put_act(264, act_of(high[8:16], high[16:24], high[24:32]))
            put_act(272, jnp.zeros((16, C), jnp.float32))
        m = 144 if last else 128
        even, odd = (
            jnp.concatenate([act_s[b, pl.ds(first, m, stride=2), :] for b in range(6)], axis=1)
            .astype(jnp.bfloat16)
            for first in (0, 1)
        )
        if step == 0:
            loads[1].wait()
        for nb in range(3):
            cols = pl.ds(nb * 512, 512)
            proj = jnp.dot(even, down[0:C, cols], preferred_element_type=jnp.float32)
            proj = proj + jnp.dot(odd, down[C:C2, cols], preferred_element_type=jnp.float32)
            panel = gelu(proj)
            for n, dest in enumerate(dests):
                for slot in range(CAP):
                    live = one_if(my_count - inv_s[dest * CAP + slot])
                    at = (n * CAP + slot) * HALF
                    outgoing[dest * CAP + slot, :, cols] = (
                        panel[at:at + HALF] * live).astype(jnp.bfloat16)
            if last:
                low_live = one_if(me) * one_if(counts_ref[0, (me + N_SEQ - 1) % N_SEQ] - (GROUPS_DEV - 1))
                high_live = one_if(N_SEQ - 1 - me) * one_if(counts_ref[0, (me + 1) % N_SEQ])
                ends = panel[128:136].astype(jnp.bfloat16).astype(jnp.float32)
                qf[4:8, cols] = ends[0:4] * low_live
                qf[520:524, cols] = ends[4:8] * high_live
        for n, (kx, kz) in enumerate(pair):
            src = outgoing.at[pl.ds(dests[n] * CAP, CAP)]
            dst = owned_ref.at[0, pl.ds(me * CAP, CAP)]
            if (kx, kz) == (0, 0):
                own = pltpu.make_async_copy(src, dst, own_sem)
                own.start()
            else:
                k = kx * 2 + kz - 1
                send = pltpu.make_async_remote_copy(
                    src, dst, a_send.at[k], a_recv.at[k],
                    device_id=(dp, dests[n]), device_id_type=MESH)
                send.start()
                sends.append(send)

    def place_rows(j, carry):
        qf[pl.ds(pl.multiple_of(8 + j * HALF, 8), HALF), :] = outgoing[place_s[j]].astype(jnp.float32)
        return carry

    lax.fori_loop(0, GROUPS_DEV, place_rows, 0)
    b0, b1, b2 = bdw_ref[0:1, :], bdw_ref[1:2, :], bdw_ref[2:3, :]

    def mix(r, carry):
        base = pl.multiple_of(r * 128, 128)
        for cb in range(6):
            cols = pl.ds(cb * 256, 256)
            v = qf[pl.ds(base, 144), cols]
            bb = slice(cb * 256, cb * 256 + 256)
            value = (b0[:, bb] * v[7:135] + b1[:, bb] * v[8:136] + b2[:, bb] * v[9:137])
            mixed[pl.ds(base, 128), cols] = value.astype(jnp.bfloat16)
            mixed_t[pl.ds(cb * 256, 256), pl.ds(base, 128)] = value.T.astype(jnp.bfloat16)
        return carry

    lax.fori_loop(0, 4, mix, 0)
    loads[2].wait()
    loads[3].wait()

    def copy_core(c):
        return pltpu.make_async_remote_copy(
            csend.at[c], crecv.at[c], c_send.at[c], c_recv.at[c],
            device_id=(dp_of(my, zh, 1 - core), me), device_id_type=MESH)

    def copy_y(c, k):
        return pltpu.make_async_remote_copy(
            ysend.at[c, k - 1], yrecv.at[c, k - 1], y_send.at[c, k - 1], y_recv.at[c, k - 1],
            device_id=(dp_of((my + k) % 4, zh, core), me), device_id_type=MESH)

    def copy_z(c, k):
        return pltpu.make_async_remote_copy(
            zsend.at[c, k - 1], zrecv.at[c, k - 1], z_send.at[c, k - 1], z_recv.at[c, k - 1],
            device_id=(dp_of(my, (zh + k) % 4, core), me), device_id_type=MESH)

    def copy_s(k):
        return pltpu.make_async_remote_copy(
            ssend.at[k], srecv.at[k - 1], s_send.at[k - 1], s_recv.at[k - 1],
            device_id=(dp, seq_at(k // 2, k % 2)), device_id_type=MESH)

    def make_term(c):
        cols = pl.ds(c * CW, CW)
        delta = []
        for r in range(4):
            rows = pl.ds(r * 128, 128)
            pre = jnp.dot(mixed[rows, :], bott[:, cols], preferred_element_type=jnp.float32)
            value, slope = gelu_both(pre)
            result[rows, cols] = value.astype(jnp.bfloat16)
            delta.append((cot[rows, cols].astype(jnp.float32) * slope).astype(jnp.bfloat16))
        delta = jnp.concatenate(delta, axis=0)
        for i in range(4):
            part = jnp.dot(mixed_t[pl.ds(i * 384, 384), :], delta, preferred_element_type=jnp.float32)
            gbuf[c, pl.ds(i * 4, 4)] = part.reshape(4, 2, 48, CW)
        csend[c] = gbuf[c, :, 1 - core].astype(jnp.bfloat16)
        copy_core(c).start()

    def after_core(c):
        copy_core(c).wait_recv()

        def summed(y):
            rows = pl.ds(y * 4, 4)
            return gbuf[c, rows, core] + crecv[c, rows].astype(jnp.float32)

        for k in (2, 1, 3):
            ysend[c, k - 1] = summed((my + k) % 4).astype(jnp.bfloat16)
            copy_y(c, k).start()
        yacc[c] = summed(my)

    def after_y(c):
        for k in (1, 2, 3):
            copy_y(c, k).wait_recv()

        def summed(z):
            total = yacc[c, z]
            for k in (1, 2, 3):
                total = total + yrecv[c, k - 1, z].astype(jnp.float32)
            return total

        for k in (2, 1, 3):
            zsend[c, k - 1] = summed((zh + k) % 4).astype(jnp.bfloat16)
            copy_z(c, k).start()
        zacc[:, pl.ds(c * CW, CW)] = summed(zh)

    def after_z(c):
        cols = pl.ds(c * CW, CW)
        total = zacc[:, cols]
        for k in (1, 2, 3):
            copy_z(c, k).wait_recv()
            total = total + zrecv[c, k - 1].astype(jnp.float32)
        for s in range(N_SEQ):
            sx, sz = s // 2, s % 2
            k = ((sx + 4 - mx) % 4) * 2 + (sz + 2 - mz) % 2
            ssend[k, 0:6, cols] = total[s * 6:s * 6 + 6]

    make_term(0)
    make_term(1)
    after_core(0)
    make_term(2)
    after_core(1)
    write = pltpu.make_async_copy(result, out_ref.at[0], out_sem)
    write.start()
    after_core(2)
    for c in range(NC):
        after_y(c)
    for c in range(NC):
        after_z(c)
    for k in (5, 4, 3, 7, 2, 6, 1):
        copy_s(k).start()
    total = ssend[0]
    for k in range(1, 8):
        copy_s(k).wait_recv()
        total = total + srecv[k - 1]
    grad_ref[...] = total[0:6]

    for send in sends:
        send.wait()
    own.wait()
    write.wait()
    for h in halos:
        h.wait_send()
    for c in range(NC):
        copy_core(c).wait_send()
        for k in (1, 2, 3):
            copy_y(c, k).wait_send()
            copy_z(c, k).wait_send()
    for k in range(1, 8):
        copy_s(k).wait_send()


def on_device(tokens, depthwise_weight, down_weight, bott_dw, bott_weight, cotangent,
              plan_owner, plan_slot, counts):
    smem = pl.BlockSpec(memory_space=pltpu.SMEM)
    vmem = pl.BlockSpec(memory_space=pltpu.VMEM)
    far = pl.BlockSpec(memory_space=pl.ANY)
    bf16, f32 = jnp.bfloat16, jnp.float32
    V, DMA = pltpu.VMEM, pltpu.SemaphoreType.DMA
    return pl.pallas_call(
        kernel,
        out_shape=(
            jax.ShapeDtypeStruct((1, GROUPS_DEV, HALF, C2), bf16),
            jax.ShapeDtypeStruct((1, HROWS, C), bf16),
            jax.ShapeDtypeStruct((6, C), f32),
        ),
        in_specs=[smem, smem, smem, far, vmem, far, vmem, far, far],
        out_specs=(far, far, vmem),
        scratch_shapes=[
            pltpu.SMEM((GROUPS_DEV,), jnp.int32),
            pltpu.SMEM((GROUPS_DEV,), jnp.int32),
            V((ROWS // PAD + 2, PAD, C), bf16),
            V((C2, C2), bf16),
            V((C2, C), bf16),
            V((HROWS, C), bf16),
            V((6, 288, 128), f32),
            V((GROUPS_DEV, HALF, C2), bf16),
            V((HROWS + 16, C2), f32),
            V((HROWS, C2), bf16),
            V((C2, HROWS), bf16),
            V((HROWS, C), bf16),
            V((NC, 16, 2, 48, CW), f32),
            V((NC, 16, 48, CW), bf16),
            V((NC, 16, 48, CW), bf16),
            V((NC, 4, 48, CW), f32),
            V((NC, 3, 4, 48, CW), bf16),
            V((NC, 3, 4, 48, CW), bf16),
            V((48, C), f32),
            V((NC, 3, 48, CW), bf16),
            V((NC, 3, 48, CW), bf16),
            V((8, 8, C), f32),
            V((7, 8, C), f32),
            DMA((4,)), DMA((2,)), DMA((2,)), DMA((7,)), DMA((7,)), DMA, DMA,
            DMA((NC,)), DMA((NC,)), DMA((NC, 3)), DMA((NC, 3)),
            DMA((NC, 3)), DMA((NC, 3)), DMA((7,)), DMA((7,)),
        ],
        compiler_params=pltpu.CompilerParams(
            collective_id=0, has_side_effects=True, vmem_limit_bytes=56 * 1024 * 1024),
        cost_estimate=pl.CostEstimate(
            flops=5_000_000_000, bytes_accessed=14_000_000, transcendentals=2_000_000),
    )(plan_owner, plan_slot, counts, tokens.reshape(ROWS // PAD, PAD, C), depthwise_weight, down_weight, bott_dw,
      bott_weight, cotangent)


def solution(mesh):
    placed = (
        P("dp", "seq", None),
        P(),
        P(),
        P(),
        P(),
        P("dp", "seq", None),
        P("dp", None),
        P("dp", None),
        P("dp", None),
    )
    return jax.shard_map(
        on_device,
        mesh=mesh,
        in_specs=placed,
        out_specs=(P("dp", "seq", None, None), P("dp", "seq", None), P(("dp", "seq"), None)),
        check_vma=False,
    )
```

```python
import jax
import jax.numpy as jnp
from jax import lax
from jax.experimental import pallas as pl
from jax.experimental.pallas import tpu as pltpu
from jax.sharding import PartitionSpec as P

C = 768
C2 = 1536
GROUP = 32
GROUPS_DEV = 32
HALF = 16
CAP = 4
N_SEQ = 8
ROWS = 1024
HROWS = 512
PAD = 16
NC = 3
CW = C // NC
MESH = pl.DeviceIdType.MESH
K0 = 0.7978845608028654
K1 = 0.044715
ORDER = (((2, 1), (2, 0)), ((1, 1), (3, 1)), ((1, 0), (3, 0)), ((0, 1), (0, 0)))
BF16, F32 = jnp.bfloat16, jnp.float32


def gelu(x):
    return 0.5 * x * (1.0 + jnp.tanh(K0 * x * (1.0 + K1 * (x * x))))


def gelu_both(x):
    square = x * x
    t = jnp.tanh(K0 * x * (1.0 + K1 * square))
    half = 0.5 * (1.0 + t)
    slope = half + 0.5 * x * (1.0 - t * t) * (K0 * (1.0 + 3.0 * K1 * square))
    return x * half, slope


def one_if(n):
    return jnp.clip(n, 0, 1).astype(F32)


def pack24(v):
    rest = v[16:24]
    return jnp.concatenate(
        [v[0:16], jnp.concatenate([rest[:, 0:128], rest[:, 128:256]], axis=0)], axis=1)


def unpack24(v):
    rest = v[:, 256:384]
    return jnp.concatenate(
        [v[:, 0:256], jnp.concatenate([rest[0:8], rest[8:16]], axis=1)], axis=0)


def pack8(v):
    return jnp.concatenate([v[:, 0:128], v[:, 128:256]], axis=0)


def unpack8(v):
    return jnp.concatenate([v[0:8], v[8:16]], axis=1)


def kernel(
    owner_ref, slot_ref, counts_ref, tokens_ref, dw_ref, down_ref, bdw_ref, bott_ref, cot_ref,
    owned_ref, out_ref, grad_ref,
    owner_s, slot_s, counts_s, place_s, inv_s, dw, bdw,
    tok, halo, down, bott, cot, act_s, pairs, outgoing, qf, mixed, mixed_t, result,
    gbuf, csend, crecv, bown, ysend, yrecv, sown, ssend, srecv, zown, zsend, zrecv,
    in_sem, halo_send, halo_recv, a_send, a_recv, own_sem, out_sem,
    c_send, c_recv, y_send, y_recv, s_send, s_recv, z_send, z_recv,
):
    dp = lax.axis_index("dp")
    me = lax.axis_index("seq")
    mx, mz = me // 2, me % 2
    core = dp % 2
    zh = (dp // 2) % 4
    my = dp // 8

    def seq_at(kx, kz):
        return ((mx + kx) % 4) * 2 + (mz + kz) % 2

    def dp_of(y, z, c):
        return y * 8 + z * 2 + c

    barrier = pltpu.get_barrier_semaphore()
    peers = [(dp, seq_at(k // 2, k % 2)) for k in range(1, 8)]
    peers += [(dp_of(my, zh, 1 - core), me)]
    peers += [(dp_of((my + k) % 4, zh, core), me) for k in (1, 3)]
    peers += [(dp_of(my, (zh + k) % 4, core), me) for k in range(1, 4)]
    for peer in peers:
        pl.semaphore_signal(barrier, inc=1, device_id=peer, device_id_type=MESH)

    loads = [
        pltpu.make_async_copy(src, dst, in_sem.at[i])
        for i, (src, dst) in enumerate((
            (tokens_ref, tok.at[pl.ds(1, 64)]), (dw_ref, dw), (owner_ref, owner_s), (slot_ref, slot_s),
            (counts_ref, counts_s), (down_ref, down), (bdw_ref, bdw), (bott_ref, bott), (cot_ref.at[0], cot),
        ))
    ]
    for load in loads:
        load.start()
    tok[0] = jnp.zeros((PAD, C), BF16)
    tok[65] = jnp.zeros((PAD, C), BF16)
    pl.semaphore_wait(barrier, len(peers))

    up, dn = (me + 1) % N_SEQ, (me + N_SEQ - 1) % N_SEQ
    halos = [
        pltpu.make_async_remote_copy(
            tokens_ref.at[63], halo.at[0],
            halo_send.at[0], halo_recv.at[0], device_id=(dp, up), device_id_type=MESH),
        pltpu.make_async_remote_copy(
            tokens_ref.at[0], halo.at[1],
            halo_send.at[1], halo_recv.at[1], device_id=(dp, dn), device_id_type=MESH),
    ]
    for h in halos:
        h.start()
    loads[0].wait()
    loads[1].wait()

    def act_of(rows, count, b):
        cols = slice(b * 128, b * 128 + 128)
        here = rows[8:8 + count, cols]
        conv = (dw[0:1, cols] * rows[0:count, cols] + dw[1:2, cols] * here
                + dw[2:3, cols] * rows[16:16 + count, cols])
        return here + gelu(conv)

    def paired(at, count, first):
        return jnp.concatenate(
            [act_s[at, b, pl.ds(first + odd, count, stride=2), :] for odd in (0, 1) for b in range(6)],
            axis=1).astype(BF16)

    def four_groups(i, carry):
        rows = tok[pl.ds(8 * i, 10)].reshape(160, C).astype(F32)[8:152]
        for b in range(6):
            act_s[0, b, 0:128, :] = act_of(rows, 128, b)
        pairs[pl.ds(4 * i, 4)] = paired(0, 64, 0).reshape(4, HALF, C2)
        return carry

    lax.fori_loop(0, 8, four_groups, 0)

    for load in loads[2:5]:
        load.wait()

    def set_place(j, carry):
        place_s[j] = owner_s[0, me * GROUPS_DEV + j] * CAP + slot_s[0, me * GROUPS_DEV + j]
        return carry

    lax.fori_loop(0, GROUPS_DEV, set_place, 0)

    def set_inv(p, carry):
        found = jnp.int32(0)
        for j in range(GROUPS_DEV):
            found = found + j * (1 - jnp.minimum(jnp.abs(place_s[j] - p), 1))
        inv_s[p] = jnp.minimum(found, GROUPS_DEV - 1)
        return carry

    lax.fori_loop(0, GROUPS_DEV, set_inv, 0)

    for h in halos:
        h.wait_recv()
    low = jnp.concatenate(
        [halo[0].astype(F32) * one_if(me), tok[1:4].reshape(48, C).astype(F32)], axis=0)
    high = jnp.concatenate(
        [tok[62:65].reshape(48, C).astype(F32), halo[1].astype(F32) * one_if(N_SEQ - 1 - me)], axis=0)
    for b in range(6):
        act_s[0, b, 0:40, :] = act_of(low, 40, b)
        act_s[1, b, 0:40, :] = act_of(high[8:64], 40, b)
    pairs[0] = paired(0, 16, 8)
    pairs[GROUPS_DEV - 1] = paired(1, 16, 0)
    zero = jnp.zeros((8, C2), BF16)
    ends = jnp.concatenate([paired(0, 4, 0), paired(1, 4, 32), zero], axis=0)

    my_count = counts_s[0, me]
    sends = []
    for step, pair in enumerate(ORDER):
        dests = [seq_at(*offset) for offset in pair]
        groups = [inv_s[dest * CAP + slot] for dest in dests for slot in range(CAP)]
        places = [dest * CAP + slot for dest in dests for slot in range(CAP)]
        last = step == len(ORDER) - 1
        rows = jnp.concatenate([pairs[group] for group in groups] + ([ends] if last else []), axis=0)
        if step == 0:
            loads[5].wait()
        for nb in range(3):
            cols = pl.ds(nb * 512, 512)
            panel = gelu(jnp.dot(rows, down[:, cols], preferred_element_type=F32))
            for n in range(8):
                live = one_if(my_count - groups[n])
                outgoing[places[n], :, cols] = (panel[n * HALF:n * HALF + HALF] * live).astype(BF16)
            if last:
                low_live = one_if(me) * one_if(counts_s[0, dn] - (GROUPS_DEV - 1))
                high_live = one_if(N_SEQ - 1 - me) * one_if(counts_s[0, up])
                beyond = panel[128:136].astype(BF16).astype(F32)
                qf[4:8, cols] = beyond[0:4] * low_live
                qf[520:524, cols] = beyond[4:8] * high_live
        for n, (kx, kz) in enumerate(pair):
            src = outgoing.at[pl.ds(dests[n] * CAP, CAP)]
            dst = owned_ref.at[0, pl.ds(me * CAP, CAP)]
            if (kx, kz) == (0, 0):
                own = pltpu.make_async_copy(src, dst, own_sem)
                own.start()
            else:
                k = kx * 2 + kz - 1
                send = pltpu.make_async_remote_copy(
                    src, dst, a_send.at[k], a_recv.at[k],
                    device_id=(dp, dests[n]), device_id_type=MESH)
                send.start()
                sends.append(send)

    def place_rows(j, carry):
        qf[pl.ds(pl.multiple_of(8 + j * HALF, 8), HALF), :] = outgoing[place_s[j]].astype(F32)
        return carry

    lax.fori_loop(0, GROUPS_DEV, place_rows, 0)
    loads[6].wait()

    def mix(r, carry):
        base = pl.multiple_of(r * 128, 128)
        for cb in range(6):
            cols = pl.ds(cb * 256, 256)
            v = qf[pl.ds(base, 144), cols]
            value = bdw[0:1, cols] * v[7:135] + bdw[1:2, cols] * v[8:136] + bdw[2:3, cols] * v[9:137]
            mixed[pl.ds(base, 128), cols] = value.astype(BF16)
            mixed_t[pl.ds(cb * 256, 256), pl.ds(base, 128)] = value.T.astype(BF16)
        return carry

    lax.fori_loop(0, 4, mix, 0)
    loads[7].wait()
    loads[8].wait()

    def remote(src, dst, send_sem, recv_sem, device):
        return pltpu.make_async_remote_copy(
            src, dst, send_sem, recv_sem, device_id=device, device_id_type=MESH)

    def copy_core(c):
        return remote(csend.at[c], crecv.at[c], c_send.at[c], c_recv.at[c], (dp_of(my, zh, 1 - core), me))

    def copy_y(c, n):
        to = (my + (1 if n < 3 else 3)) % 4
        return remote(ysend.at[c, n], yrecv.at[c, n], y_send.at[c, n], y_recv.at[c, n],
                      (dp_of(to, zh, core), me))

    def copy_s(c, k):
        return remote(ssend.at[c, k], srecv.at[c, k - 1], s_send.at[c, k - 1], s_recv.at[c, k - 1],
                      (dp, seq_at(k // 2, k % 2)))

    def copy_z(c, k):
        return remote(zsend.at[c, k], zrecv.at[c, k - 1], z_send.at[c, k - 1], z_recv.at[c, k - 1],
                      (dp_of(my, (zh + k) % 4, core), me))

    def make_term(c):
        cols = pl.ds(c * CW, CW)
        delta = []
        for r in range(4):
            rows = pl.ds(r * 128, 128)
            pre = jnp.dot(mixed[rows, :], bott[:, cols], preferred_element_type=F32)
            value, slope = gelu_both(pre)
            result[rows, cols] = value.astype(BF16)
            delta.append((cot[rows, cols].astype(F32) * slope).astype(BF16))
        delta = jnp.concatenate(delta, axis=0)
        for i in range(4):
            part = jnp.dot(mixed_t[pl.ds(i * 384, 384), :], delta, preferred_element_type=F32)
            gbuf[c, pl.ds(i * 4, 4)] = part.reshape(4, 2, 48, CW)
        csend[c] = gbuf[c, :, 1 - core].astype(BF16)
        copy_core(c).start()

    def after_core(c):
        copy_core(c).wait_recv()

        def summed(y, half):
            rows = pl.ds(y * 4 + half * 2, 2)
            return gbuf[c, rows, core] + crecv[c, rows].astype(F32)

        nxt, across, prv = (my + 1) % 4, (my + 2) % 4, (my + 3) % 4
        for n, block, half in ((0, across, 0), (3, across, 1), (1, nxt, 1), (4, prv, 0)):
            ysend[c, n] = summed(block, half).astype(BF16)
            copy_y(c, n).start()
        bown[c, 0] = summed(nxt, 0)
        bown[c, 1] = summed(prv, 1)
        bown[c, 2] = summed(my, 0)
        bown[c, 3] = summed(my, 1)

    def pass_y(c):
        copy_y(c, 0).wait_recv()
        ysend[c, 2] = (bown[c, 0] + yrecv[c, 0].astype(F32)).astype(BF16)
        copy_y(c, 2).start()
        copy_y(c, 3).wait_recv()
        ysend[c, 5] = (bown[c, 1] + yrecv[c, 3].astype(F32)).astype(BF16)
        copy_y(c, 5).start()

    def after_y(c):
        for n in (1, 4, 2, 5):
            copy_y(c, n).wait_recv()
        half0 = bown[c, 2] + yrecv[c, 2].astype(F32) + yrecv[c, 4].astype(F32)
        half1 = bown[c, 3] + yrecv[c, 1].astype(F32) + yrecv[c, 5].astype(F32)
        blocks = (half0[0], half0[1], half1[0], half1[1])
        for s in range(N_SEQ):
            k = ((s // 2 + 4 - mx) % 4) * 2 + (s % 2 + 2 - mz) % 2
            part = jnp.concatenate([block[s * 6:s * 6 + 6] for block in blocks], axis=0)
            part = pack24(part)
            sown[c, k] = part
            ssend[c, k] = part.astype(BF16)
        for k in (5, 4, 3, 7, 2, 6, 1):
            copy_s(c, k).start()

    def after_s(c):
        total = sown[c, 0]
        for k in range(1, 8):
            copy_s(c, k).wait_recv()
            total = total + srecv[c, k - 1].astype(F32)
        total = unpack24(total)
        for z in range(4):
            k = (z + 4 - zh) % 4
            part = jnp.concatenate([total[z * 6:z * 6 + 6], jnp.zeros((2, CW), F32)], axis=0)
            zown[c, k] = part
            zsend[c, k] = pack8(part).astype(BF16)
        for k in (2, 1, 3):
            copy_z(c, k).start()

    def after_z(c):
        total = zown[c, 0]
        for k in (1, 2, 3):
            copy_z(c, k).wait_recv()
            total = total + unpack8(zrecv[c, k - 1].astype(F32))
        grad_ref[:, c * CW:c * CW + CW] = total[0:6]

    make_term(0)
    make_term(1)
    after_core(0)
    make_term(2)
    after_core(1)
    pass_y(0)
    write = pltpu.make_async_copy(result, out_ref.at[0], out_sem)
    write.start()
    after_core(2)
    pass_y(1)
    after_y(0)
    pass_y(2)
    after_y(1)
    after_s(0)
    after_y(2)
    after_s(1)
    after_s(2)
    for c in range(NC):
        after_z(c)

    for send in sends:
        send.wait()
    own.wait()
    write.wait()
    for h in halos:
        h.wait_send()
    for c in range(NC):
        copy_core(c).wait_send()
        for n in range(6):
            copy_y(c, n).wait_send()
        for k in range(1, 8):
            copy_s(c, k).wait_send()
        for k in range(1, 4):
            copy_z(c, k).wait_send()


OUTS = (
    jax.ShapeDtypeStruct((1, GROUPS_DEV, HALF, C2), BF16),
    jax.ShapeDtypeStruct((1, HROWS, C), BF16),
    jax.ShapeDtypeStruct((6, C), F32),
)
FAR = pl.BlockSpec(memory_space=pl.ANY)


def hand_over(owned_ref, out_ref, grad_ref, owned_to, out_to, grad_to, sems):
    copies = [pltpu.make_async_copy(grad_ref, grad_to, sems.at[0])]
    for i in range(4):
        rows = pl.ds(i * 8, 8)
        copies.append(pltpu.make_async_copy(owned_ref.at[0, rows], owned_to.at[0, rows], sems.at[1 + i]))
    for i in range(2):
        rows = pl.ds(i * 256, 256)
        copies.append(pltpu.make_async_copy(out_ref.at[0, rows], out_to.at[0, rows], sems.at[5 + i]))
    for copy in copies:
        copy.start()
    for copy in copies:
        copy.wait()


def on_device(tokens, depthwise_weight, down_weight, bott_dw, bott_weight, cotangent,
              plan_owner, plan_slot, counts):
    V, S, DMA = pltpu.VMEM, pltpu.SMEM, pltpu.SemaphoreType.DMA
    made = pl.pallas_call(
        kernel,
        out_shape=tuple(pltpu.VMEM(o.shape, o.dtype) for o in OUTS),
        in_specs=[FAR] * 9,
        out_specs=(pl.BlockSpec(memory_space=pltpu.VMEM),) * 3,
        scratch_shapes=[
            S((1, 256), jnp.int32),
            S((1, 256), jnp.int32),
            S((1, 8), jnp.int32),
            S((GROUPS_DEV,), jnp.int32),
            S((GROUPS_DEV,), jnp.int32),
            V((3, C), F32),
            V((3, C2), F32),
            V((ROWS // PAD + 2, PAD, C), BF16),
            V((2, PAD, C), BF16),
            V((C2, C2), BF16),
            V((C2, C), BF16),
            V((HROWS, C), BF16),
            V((2, 6, 128, 128), F32),
            V((GROUPS_DEV, HALF, C2), BF16),
            V((GROUPS_DEV, HALF, C2), BF16),
            V((HROWS + 16, C2), F32),
            V((HROWS, C2), BF16),
            V((C2, HROWS), BF16),
            V((HROWS, C), BF16),
            V((NC, 16, 2, 48, CW), F32),
            V((NC, 16, 48, CW), BF16),
            V((NC, 16, 48, CW), BF16),
            V((NC, 4, 2, 48, CW), F32),
            V((NC, 6, 2, 48, CW), BF16),
            V((NC, 6, 2, 48, CW), BF16),
            V((NC, 8, 16, 384), F32),
            V((NC, 8, 16, 384), BF16),
            V((NC, 7, 16, 384), BF16),
            V((NC, 4, 8, CW), F32),
            V((NC, 4, 16, 128), BF16),
            V((NC, 3, 16, 128), BF16),
            DMA((9,)), DMA((2,)), DMA((2,)), DMA((7,)), DMA((7,)), DMA, DMA,
            DMA((NC,)), DMA((NC,)), DMA((NC, 6)), DMA((NC, 6)),
            DMA((NC, 7)), DMA((NC, 7)), DMA((NC, 3)), DMA((NC, 3)),
        ],
        compiler_params=pltpu.CompilerParams(
            collective_id=0, has_side_effects=True, vmem_limit_bytes=56 * 1024 * 1024),
        cost_estimate=pl.CostEstimate(
            flops=5_000_000_000, bytes_accessed=14_000_000, transcendentals=2_000_000),
    )(plan_owner, plan_slot, counts, tokens.reshape(ROWS // PAD, PAD, C), depthwise_weight, down_weight,
      bott_dw, bott_weight, cotangent)
    return pl.pallas_call(
        hand_over,
        out_shape=OUTS,
        in_specs=[FAR] * 3,
        out_specs=(FAR,) * 3,
        scratch_shapes=[DMA((7,))],
        compiler_params=pltpu.CompilerParams(vmem_limit_bytes=40 * 1024 * 1024),
    )(*made)


def solution(mesh):
    placed = (
        P("dp", "seq", None),
        P(),
        P(),
        P(),
        P(),
        P("dp", "seq", None),
        P("dp", None),
        P("dp", None),
        P("dp", None),
    )
    return jax.shard_map(
        on_device,
        mesh=mesh,
        in_specs=placed,
        out_specs=(P("dp", "seq", None, None), P("dp", "seq", None), P(("dp", "seq"), None)),
        check_vma=False,
    )
```

```python
import jax
import jax.numpy as jnp
from jax import lax
from jax.experimental import pallas as pl
from jax.experimental.pallas import tpu as pltpu
from jax.sharding import PartitionSpec as P

C = 768
C2 = 1536
GROUP = 32
GROUPS_DEV = 32
HALF = 16
CAP = 4
N_SEQ = 8
ROWS = 1024
HROWS = 512
PAD = 16
NC = 3
CW = C // NC
MESH = pl.DeviceIdType.MESH
K0 = 0.7978845608028654
K1 = 0.044715
ORDER = (((2, 1), (1, 1), (3, 1), (0, 1), (2, 0), (1, 0), (3, 0), (0, 0)), (), (), (), ())
BF16, F32 = jnp.bfloat16, jnp.float32


def gelu(x):
    return 0.5 * x * (1.0 + jnp.tanh(K0 * x * (1.0 + K1 * (x * x))))


def gelu_both(x):
    square = x * x
    t = jnp.tanh(K0 * x * (1.0 + K1 * square))
    half = 0.5 * (1.0 + t)
    slope = half + 0.5 * x * (1.0 - t * t) * (K0 * (1.0 + 3.0 * K1 * square))
    return x * half, slope


def one_if(n):
    return jnp.clip(n, 0, 1).astype(F32)


def pack8(v):
    v = jnp.concatenate([v, jnp.zeros((2, v.shape[1]), F32)], axis=0)
    if v.shape[1] == 128:
        return jnp.concatenate([v, jnp.zeros((8, 128), F32)], axis=0)
    return jnp.concatenate([v[:, 0:128], v[:, 128:256]], axis=0)


def unpack8(v, width):
    if width == 128:
        return v[0:6]
    return jnp.concatenate([v[0:6], v[8:14]], axis=1)


def kernel(
    owner_ref, slot_ref, counts_ref, tokens_ref, dw_ref, down_ref, bdw_ref, bott_ref, cot_ref,
    owned_ref, out_ref, grad_ref,
    owner_s, slot_s, counts_s, amount_s, inv_s, dw, bdw,
    tok, halo, down, bott, cot, act_s, pairs, panels, outgoing, qf, mixed, mixed_t,
    gbuf, csend, crecv, chunk_bufs,
    in_sem, halo_send, halo_recv, a_send, a_recv, own_sem,
    c_send, c_recv, chunk_sems,
):
    dp = lax.axis_index("dp")
    me = lax.axis_index("seq")
    mx, mz = me // 2, me % 2
    core = dp % 2
    zh = (dp // 2) % 4
    my = dp // 8

    def seq_at(kx, kz):
        return ((mx + kx) % 4) * 2 + (mz + kz) % 2

    def dp_of(y, z, c):
        return y * 8 + z * 2 + c

    loads = [
        pltpu.make_async_copy(src, dst, in_sem.at[i])
        for i, (src, dst) in enumerate((
            (tokens_ref, tok.at[pl.ds(1, 64)]), (dw_ref, dw), (owner_ref, owner_s), (slot_ref, slot_s),
            (counts_ref, counts_s), (down_ref, down), (bdw_ref, bdw), (bott_ref, bott), (cot_ref.at[0], cot),
        ))
    ]
    for load in loads[0:6]:
        load.start()
    barrier = pltpu.get_barrier_semaphore()
    peers = [(dp, seq_at(k // 2, k % 2)) for k in range(1, 8)]
    peers += [(dp_of(my, zh, 1 - core), me)]
    peers += [(dp_of((my + k) % 4, zh, core), me) for k in range(1, 4)]
    peers += [(dp_of(my, (zh + k) % 4, core), mx * 2 + z) for k in range(1, 4) for z in range(2)]
    for peer in peers:
        pl.semaphore_signal(barrier, inc=1, device_id=peer, device_id_type=MESH)

    tok[0] = jnp.zeros((PAD, C), BF16)
    tok[65] = jnp.zeros((PAD, C), BF16)
    pl.semaphore_wait(barrier, len(peers))

    up, dn = (me + 1) % N_SEQ, (me + N_SEQ - 1) % N_SEQ
    halos = [
        pltpu.make_async_remote_copy(
            tokens_ref.at[63], halo.at[0],
            halo_send.at[0], halo_recv.at[0], device_id=(dp, up), device_id_type=MESH),
        pltpu.make_async_remote_copy(
            tokens_ref.at[0], halo.at[1],
            halo_send.at[1], halo_recv.at[1], device_id=(dp, dn), device_id_type=MESH),
    ]
    for h in halos:
        h.start()

    loads[0].wait()
    loads[1].wait()

    def act_of(rows, count, b):
        cols = slice(b * 128, b * 128 + 128)
        here = rows[8:8 + count, cols]
        conv = (dw[0:1, cols] * rows[0:count, cols] + dw[1:2, cols] * here
                + dw[2:3, cols] * rows[16:16 + count, cols])
        return here + gelu(conv)

    def paired(at, count, first):
        return jnp.concatenate(
            [act_s[at, b, pl.ds(first + odd, count, stride=2), :] for odd in (0, 1) for b in range(6)],
            axis=1).astype(BF16)

    def four_groups(i):
        at = i % 2
        rows = tok[8 * i:8 * i + 10].reshape(160, C).astype(F32)[8:152]
        for b in range(6):
            act_s[at, b, 0:128, :] = act_of(rows, 128, b)
        pairs[4 * i:4 * i + 4] = paired(at, 64, 0).reshape(4, HALF, C2)


    def project(first, beside, ends=None):
        rows = pairs[first:first + 8].reshape(128, C2)
        if ends is not None:
            rows = jnp.concatenate([rows, ends], axis=0)
        for nb in range(3):
            cols = pl.ds(nb * 512, 512)
            panel = gelu(jnp.dot(rows, down[:, cols], preferred_element_type=F32))
            for n in range(8):
                value = (panel[n * HALF:n * HALF + HALF] * one_if(my_count - (first + n))).astype(BF16)
                panels[first + n, :, cols] = value
                qf[8 + (first + n) * HALF:8 + (first + n + 1) * HALF, cols] = value.astype(F32)
            if ends is not None:
                low_live = one_if(me) * one_if(counts_s[0, dn] - (GROUPS_DEV - 1))
                high_live = one_if(N_SEQ - 1 - me) * one_if(counts_s[0, up])
                beyond = panel[128:136].astype(BF16).astype(F32)
                qf[4:8, cols] = beyond[0:4] * low_live
                qf[520:524, cols] = beyond[4:8] * high_live
            if nb < len(beside):
                four_groups(beside[nb])

    for i in (2, 3, 4, 5):
        four_groups(i)

    for load in loads[2:5]:
        load.wait()

    def set_amount(j, carry):
        slot = slot_s[0, me * GROUPS_DEV + j]
        weight = (1 + 255 * jnp.minimum(slot, 1)) * (1 + 255 * jnp.clip(slot - 1, 0, 1)) * (
            1 + 255 * jnp.clip(slot - 2, 0, 1))
        amount_s[j] = j * weight
        return carry

    lax.fori_loop(0, GROUPS_DEV, set_amount, 0)

    def set_inv(d, carry):
        held = jnp.int32(0)
        for j in range(GROUPS_DEV):
            away = jnp.abs(owner_s[0, me * GROUPS_DEV + j] - d)
            held = held + amount_s[j] * (1 - jnp.minimum(away, 1))
        for slot in range(CAP):
            inv_s[d * CAP + slot] = jnp.minimum((held // 256 ** slot) % 256, GROUPS_DEV - 1)
        return carry

    lax.fori_loop(0, N_SEQ, set_inv, 0)
    my_count = counts_s[0, me]
    loads[5].wait()
    for load in loads[6:]:
        load.start()
    project(8, (0, 1))
    project(16, (6, 7))

    for h in halos:
        h.wait_recv()
    low = jnp.concatenate(
        [halo[0].astype(F32) * one_if(me), tok[1:4].reshape(48, C).astype(F32)], axis=0)
    high = jnp.concatenate(
        [tok[62:65].reshape(48, C).astype(F32), halo[1].astype(F32) * one_if(N_SEQ - 1 - me)], axis=0)
    for b in range(6):
        act_s[0, b, 0:40, :] = act_of(low, 40, b)
        act_s[1, b, 0:40, :] = act_of(high[8:64], 40, b)
    pairs[0] = paired(0, 16, 8)
    pairs[GROUPS_DEV - 1] = paired(1, 16, 0)
    zero = jnp.zeros((8, C2), BF16)
    ends = jnp.concatenate([paired(0, 4, 0), paired(1, 4, 32), zero], axis=0)
    project(0, ())
    project(24, (), ends)

    sends, kept = [], []

    def relay(offsets):
        for kx, kz in offsets:
            dest = seq_at(kx, kz)
            for slot in range(CAP):
                outgoing[dest * CAP + slot] = panels[inv_s[dest * CAP + slot]]
            src = outgoing.at[pl.ds(dest * CAP, CAP)]
            dst = owned_ref.at[0, pl.ds(me * CAP, CAP)]
            if (kx, kz) == (0, 0):
                own = pltpu.make_async_copy(src, dst, own_sem)
                own.start()
                kept.append(own)
            else:
                k = kx * 2 + kz - 1
                send = pltpu.make_async_remote_copy(
                    src, dst, a_send.at[k], a_recv.at[k],
                    device_id=(dp, dest), device_id_type=MESH)
                send.start()
                sends.append(send)

    relay(ORDER[0])

    loads[6].wait()
    loads[7].wait()
    loads[8].wait()

    def mix(r):
        base = r * 128
        for cb in range(6):
            cols = pl.ds(cb * 256, 256)
            v = qf[base:base + 144, cols]
            value = bdw[0:1, cols] * v[7:135] + bdw[1:2, cols] * v[8:136] + bdw[2:3, cols] * v[9:137]
            value = value.astype(BF16)
            mixed[base:base + 128, cols] = value
            mixed_t[pl.ds(cb * 256, 256), base:base + 128] = value.T

    def remote(src, dst, send_sem, recv_sem, device):
        return pltpu.make_async_remote_copy(
            src, dst, send_sem, recv_sem, device_id=device, device_id_type=MESH)

    def copy_core(c):
        return remote(csend.at[c], crecv.at[c], c_send.at[c], c_recv.at[c], (dp_of(my, zh, 1 - core), me))

    def make_term(c):
        cols = pl.ds(c * CW, CW)
        delta = []
        for r in range(4):
            if c == 0:
                mix(r)
            rows = pl.ds(r * 128, 128)
            pre = jnp.dot(mixed[rows, :], bott[:, cols], preferred_element_type=F32)
            value, slope = gelu_both(pre)
            out_ref[0, rows, cols] = value.astype(BF16)
            delta.append((cot[rows, cols].astype(F32) * slope).astype(BF16))
        delta = jnp.concatenate(delta, axis=0)
        for i in range(4):
            part = jnp.dot(mixed_t[pl.ds(i * 384, 384), :], delta, preferred_element_type=F32)
            gbuf[c, pl.ds(i * 4, 4)] = part.reshape(4, 2, 48, CW)
        csend[c] = gbuf[c, :, 1 - core].astype(BF16)
        copy_core(c).start()

    def core_sum(start, width, blocks, count):
        c, lanes = start // CW, pl.ds(start % CW, width)
        rows = pl.ds(blocks, count)
        return gbuf[c, rows, core, :, lanes] + crecv[c, rows, :, lanes].astype(F32)

    class Chunk:
        def __init__(self, n):
            self.start, self.width, self.direct = CHUNKS[n]
            (self.bown, self.ysend, self.yrecv, self.xacc, self.xsend, self.xrecv,
             self.zown, self.zsend, self.zrecv) = chunk_bufs[n]
            self.sems = chunk_sems[n]

        def copy_y(self, n):
            if self.direct:
                src, dst = self.ysend.at[pl.ds(2 * n, 2)], self.yrecv.at[pl.ds(2 * n, 2)]
                to = (my + n + 1) % 4
            else:
                src, dst = self.ysend.at[n], self.yrecv.at[n]
                to = (my + (1 if n < 3 else 3)) % 4
            return remote(src, dst, self.sems[0].at[n], self.sems[1].at[n], (dp_of(to, zh, core), me))

        def copy_x(self, k):
            return remote(self.xsend.at[k - 1], self.xrecv.at[k - 1], self.sems[2].at[k - 1], self.sems[3].at[k - 1],
                          (dp, seq_at(k, 0)))

        def copy_z(self, k):
            to = (dp_of(my, (zh + k // 2) % 4, core), mx * 2 + (mz + k % 2) % 2)
            return remote(self.zsend.at[k], self.zrecv.at[k - 1], self.sems[4].at[k - 1], self.sems[5].at[k - 1], to)

        def begin(self):
            def summed(y, half):
                return core_sum(self.start, self.width, y * 4 + half * 2, 2)

            if self.direct:
                for n in (1, 0, 2):
                    for half in (0, 1):
                        self.ysend[2 * n + half] = summed((my + n + 1) % 4, half).astype(BF16)
                    self.copy_y(n).start()
                self.bown[2] = summed(my, 0)
                self.bown[3] = summed(my, 1)
                return
            nxt, across, prv = (my + 1) % 4, (my + 2) % 4, (my + 3) % 4
            for n, block, half in ((0, across, 0), (3, across, 1), (1, nxt, 1), (4, prv, 0)):
                self.ysend[n] = summed(block, half).astype(BF16)
                self.copy_y(n).start()
            self.bown[0] = summed(nxt, 0)
            self.bown[1] = summed(prv, 1)
            self.bown[2] = summed(my, 0)
            self.bown[3] = summed(my, 1)

        def pass_y(self):
            if self.direct:
                return
            self.copy_y(0).wait_recv()
            self.ysend[2] = (self.bown[0] + self.yrecv[0].astype(F32)).astype(BF16)
            self.copy_y(2).start()
            self.copy_y(3).wait_recv()
            self.ysend[5] = (self.bown[1] + self.yrecv[3].astype(F32)).astype(BF16)
            self.copy_y(5).start()

        def after_y(self):
            if self.direct:
                for n in range(3):
                    self.copy_y(n).wait_recv()
                slots = (0, 2, 4), (1, 3, 5)
            else:
                for n in (1, 4, 2, 5):
                    self.copy_y(n).wait_recv()
                slots = (2, 4), (1, 5)
            half0, half1 = self.bown[2], self.bown[3]
            for n in slots[0]:
                half0 = half0 + self.yrecv[n].astype(F32)
            for n in slots[1]:
                half1 = half1 + self.yrecv[n].astype(F32)
            for h in range(2):
                self.xacc[h] = half0[h].reshape(4, 12, self.width)
                self.xacc[2 + h] = half1[h].reshape(4, 12, self.width)
            for k in (2, 1, 3):
                part = self.xacc[:, (mx + k) % 4]
                self.xsend[k - 1] = part.reshape(48, self.width).astype(BF16)
                self.copy_x(k).start()

        def after_x(self):
            total = self.xacc[:, mx].reshape(48, self.width)
            for k in range(1, 4):
                self.copy_x(k).wait_recv()
                total = total + self.xrecv[k - 1].astype(F32)
            for z in range(8):
                k = ((z // 2 + 4 - zh) % 4) * 2 + (z % 2 + 2 - mz) % 2
                part = pack8(total[z * 6:z * 6 + 6])
                self.zown[k] = part
                self.zsend[k] = part.astype(BF16)
            for k in (4, 5, 3, 7, 2, 6, 1):
                self.copy_z(k).start()

        def after_z(self):
            total = self.zown[0]
            for k in range(1, 8):
                self.copy_z(k).wait_recv()
                total = total + self.zrecv[k - 1].astype(F32)
            grad_ref[:, self.start:self.start + self.width] = unpack8(total, self.width)

        def finish(self):
            for n in range(3 if self.direct else 6):
                self.copy_y(n).wait_send()
            for k in range(1, 4):
                self.copy_x(k).wait_send()
            for k in range(1, 8):
                self.copy_z(k).wait_send()

    chunks = [Chunk(n) for n in range(len(CHUNKS))]
    early, middle, late = ([x for x in chunks if x.start // CW == c] for c in range(NC))

    def each(part, step):
        for x in part:
            getattr(x, step)()

    make_term(0)
    relay(ORDER[1])
    make_term(1)
    copy_core(0).wait_recv()
    each(early, "begin")
    relay(ORDER[2])
    make_term(2)
    copy_core(1).wait_recv()
    each(middle, "begin")
    relay(ORDER[3])
    each(early, "pass_y")
    copy_core(2).wait_recv()
    each(late, "begin")
    relay(ORDER[4])
    each(middle, "pass_y")
    each(early, "after_y")
    each(late, "pass_y")
    each(middle, "after_y")
    each(early, "after_x")
    each(late, "after_y")
    each(middle, "after_x")
    each(late, "after_x")
    each(chunks, "after_z")

    for send in sends:
        send.wait()
    kept[0].wait()
    for h in halos:
        h.wait_send()
    for c in range(NC):
        copy_core(c).wait_send()
    each(chunks, "finish")


CHUNKS = ((0, 256, False), (256, 256, False), (512, 256, False))


def chunk_buffers(width):
    V = pltpu.VMEM
    return (
        V((4, 2, 48, width), F32), V((6, 2, 48, width), BF16), V((6, 2, 48, width), BF16),
        V((4, 4, 12, width), F32), V((3, 48, width), BF16), V((3, 48, width), BF16),
        V((8, 16, 128), F32), V((8, 16, 128), BF16), V((7, 16, 128), BF16),
    )


OUTS = (
    jax.ShapeDtypeStruct((1, GROUPS_DEV, HALF, C2), BF16),
    jax.ShapeDtypeStruct((1, HROWS, C), BF16),
    jax.ShapeDtypeStruct((6, C), F32),
)
FAR = pl.BlockSpec(memory_space=pl.ANY)


def hand_over(owned_ref, out_ref, grad_ref, owned_to, out_to, grad_to, sems):
    copies = [pltpu.make_async_copy(grad_ref, grad_to, sems.at[0])]
    for i in range(4):
        rows = pl.ds(i * 8, 8)
        copies.append(pltpu.make_async_copy(owned_ref.at[0, rows], owned_to.at[0, rows], sems.at[1 + i]))
    for i in range(2):
        rows = pl.ds(i * 256, 256)
        copies.append(pltpu.make_async_copy(out_ref.at[0, rows], out_to.at[0, rows], sems.at[5 + i]))
    for copy in copies:
        copy.start()
    for copy in copies:
        copy.wait()


def on_device(tokens, depthwise_weight, down_weight, bott_dw, bott_weight, cotangent,
              plan_owner, plan_slot, counts):
    V, S, DMA = pltpu.VMEM, pltpu.SMEM, pltpu.SemaphoreType.DMA
    made = pl.pallas_call(
        kernel,
        out_shape=tuple(pltpu.VMEM(o.shape, o.dtype) for o in OUTS),
        in_specs=[FAR] * 9,
        out_specs=(pl.BlockSpec(memory_space=pltpu.VMEM),) * 3,
        scratch_shapes=[
            S((1, 256), jnp.int32),
            S((1, 256), jnp.int32),
            S((1, 8), jnp.int32),
            S((GROUPS_DEV,), jnp.int32),
            S((GROUPS_DEV,), jnp.int32),
            V((3, C), F32),
            V((3, C2), F32),
            V((ROWS // PAD + 2, PAD, C), BF16),
            V((2, PAD, C), BF16),
            V((C2, C2), BF16),
            V((C2, C), BF16),
            V((HROWS, C), BF16),
            V((2, 6, 128, 128), F32),
            V((GROUPS_DEV, HALF, C2), BF16),
            V((GROUPS_DEV, HALF, C2), BF16),
            V((GROUPS_DEV, HALF, C2), BF16),
            V((HROWS + 16, C2), F32),
            V((HROWS, C2), BF16),
            V((C2, HROWS), BF16),
            V((NC, 16, 2, 48, CW), F32),
            V((NC, 16, 48, CW), BF16),
            V((NC, 16, 48, CW), BF16),
            tuple(chunk_buffers(width) for _, width, _ in CHUNKS),
            DMA((9,)), DMA((2,)), DMA((2,)), DMA((7,)), DMA((7,)), DMA,
            DMA((NC,)), DMA((NC,)),
            tuple((DMA((6,)), DMA((6,)), DMA((3,)), DMA((3,)), DMA((7,)), DMA((7,))) for _ in CHUNKS),
        ],
        compiler_params=pltpu.CompilerParams(
            collective_id=0, has_side_effects=True, vmem_limit_bytes=56 * 1024 * 1024),
        cost_estimate=pl.CostEstimate(
            flops=5_000_000_000, bytes_accessed=14_000_000, transcendentals=2_000_000),
    )(plan_owner, plan_slot, counts, tokens.reshape(ROWS // PAD, PAD, C), depthwise_weight, down_weight,
      bott_dw, bott_weight, cotangent)
    return pl.pallas_call(
        hand_over,
        out_shape=OUTS,
        in_specs=[FAR] * 3,
        out_specs=(FAR,) * 3,
        scratch_shapes=[DMA((7,))],
        compiler_params=pltpu.CompilerParams(vmem_limit_bytes=40 * 1024 * 1024),
    )(*made)


def solution(mesh):
    placed = (
        P("dp", "seq", None),
        P(),
        P(),
        P(),
        P(),
        P("dp", "seq", None),
        P("dp", None),
        P("dp", None),
        P("dp", None),
    )
    return jax.shard_map(
        on_device,
        mesh=mesh,
        in_specs=placed,
        out_specs=(P("dp", "seq", None, None), P("dp", "seq", None), P(("dp", "seq"), None)),
        check_vma=False,
    )
```

```python
import jax
import jax.numpy as jnp
from jax import lax
from jax.experimental import pallas as pl
from jax.experimental.pallas import tpu as pltpu
from jax.sharding import PartitionSpec as P

C = 768
C2 = 1536
GROUP = 32
GROUPS_DEV = 32
HALF = 16
CAP = 4
N_SEQ = 8
ROWS = 1024
HROWS = 512
PAD = 16
NC = 3
CW = C // NC
MESH = pl.DeviceIdType.MESH
K0 = 0.7978845608028654
K1 = 0.044715
ORDER = ((2, 1), (1, 1), (3, 1), (0, 1), (2, 0), (1, 0), (3, 0))
BF16, F32 = jnp.bfloat16, jnp.float32


def gelu(x):
    half = 0.5 * x
    return half + half * jnp.tanh(x * (K0 + (K0 * K1) * (x * x)))


def gelu_both(x):
    square = x * x
    t = jnp.tanh(x * (K0 + (K0 * K1) * square))
    half = 0.5 + 0.5 * t
    slope = half + 0.5 * x * (1.0 - t * t) * (K0 + (3.0 * K0 * K1) * square)
    return x * half, slope


def one_if(n):
    return jnp.clip(n, 0, 1).astype(F32)


def pack8(v):
    v = jnp.concatenate([v, jnp.zeros((2, v.shape[1]), F32)], axis=0)
    if v.shape[1] == 128:
        return jnp.concatenate([v, jnp.zeros((8, 128), F32)], axis=0)
    return jnp.concatenate([v[:, 0:128], v[:, 128:256]], axis=0)


def unpack8(v, width):
    if width == 128:
        return v[0:6]
    return jnp.concatenate([v[0:6], v[8:14]], axis=1)


def kernel(
    owner_ref, slot_ref, counts_ref, tokens_ref, dw_ref, down_ref, bdw_ref, bott_ref, cot_ref,
    owned_ref, out_ref, grad_ref,
    owner_s, slot_s, counts_s, amount_s, inv_s, dw, bdw,
    tok, halo, down, bott, cot, act_s, pairs, panels, outgoing, arrived, qf, mixed, mixed_t,
    gbuf, csend, crecv, chunk_bufs,
    in_sem, halo_send, halo_recv, a_send, a_recv,
    c_send, c_recv, chunk_sems,
):
    dp = lax.axis_index("dp")
    me = lax.axis_index("seq")
    mx, mz = me // 2, me % 2
    core = dp % 2
    zh = (dp // 2) % 4
    my = dp // 8

    def seq_at(kx, kz):
        return ((mx + kx) % 4) * 2 + (mz + kz) % 2

    def dp_of(y, z, c):
        return y * 8 + z * 2 + c

    loads = [
        pltpu.make_async_copy(src, dst, in_sem.at[i])
        for i, (src, dst) in enumerate((
            (tokens_ref, tok.at[pl.ds(1, 64)]), (dw_ref, dw), (owner_ref, owner_s), (slot_ref, slot_s),
            (counts_ref, counts_s), (down_ref, down), (bdw_ref, bdw), (bott_ref, bott), (cot_ref.at[0], cot),
        ))
    ]
    for load in loads[0:6]:
        load.start()
    barrier = pltpu.get_barrier_semaphore()
    peers = [(dp, seq_at(k // 2, k % 2)) for k in range(1, 8)]
    peers += [(dp_of(my, zh, 1 - core), me)]
    peers += [(dp_of((my + k) % 4, zh, core), me) for k in range(1, 4)]
    peers += [(dp_of(my, (zh + k) % 4, core), mx * 2 + z) for k in range(1, 4) for z in range(2)]
    for peer in peers:
        pl.semaphore_signal(barrier, inc=1, device_id=peer, device_id_type=MESH)

    tok[0] = jnp.zeros((PAD, C), BF16)
    tok[65] = jnp.zeros((PAD, C), BF16)
    pl.semaphore_wait(barrier, len(peers))

    up, dn = (me + 1) % N_SEQ, (me + N_SEQ - 1) % N_SEQ
    halos = [
        pltpu.make_async_remote_copy(
            tokens_ref.at[63], halo.at[0],
            halo_send.at[0], halo_recv.at[0], device_id=(dp, up), device_id_type=MESH),
        pltpu.make_async_remote_copy(
            tokens_ref.at[0], halo.at[1],
            halo_send.at[1], halo_recv.at[1], device_id=(dp, dn), device_id_type=MESH),
    ]
    for h in halos:
        h.start()

    loads[0].wait()
    loads[1].wait()

    def act_of(rows, count, b):
        cols = slice(b * 128, b * 128 + 128)
        here = rows[8:8 + count, cols]
        conv = (dw[0:1, cols] * rows[0:count, cols] + dw[1:2, cols] * here
                + dw[2:3, cols] * rows[16:16 + count, cols])
        return here + gelu(conv)

    def paired(at, count, first):
        return jnp.concatenate(
            [act_s[at, b, pl.ds(first + odd, count, stride=2), :] for odd in (0, 1) for b in range(6)],
            axis=1).astype(BF16)

    def four_groups(i):
        at = i % 2
        rows = tok[8 * i:8 * i + 10].reshape(160, C).astype(F32)[8:152]
        for b in range(6):
            act_s[at, b, 0:128, :] = act_of(rows, 128, b)
        pairs[4 * i:4 * i + 4] = paired(at, 64, 0).reshape(4, HALF, C2)


    def put_q(nb, at, value):
        for b in range(4):
            qf[nb * 4 + b, at:at + value.shape[0], :] = value[:, b * 128:b * 128 + 128]

    def project(first, beside, ends=None):
        rows = pairs[first:first + 8].reshape(128, C2)
        if ends is not None:
            rows = jnp.concatenate([rows, ends], axis=0)
        for nb in range(3):
            cols = pl.ds(nb * 512, 512)
            panel = gelu(jnp.dot(rows, down[:, cols], preferred_element_type=F32))
            for n in range(8):
                value = (panel[n * HALF:n * HALF + HALF] * one_if(my_count - (first + n))).astype(BF16)
                panels[first + n, :, cols] = value
                put_q(nb, 8 + (first + n) * HALF, value.astype(F32))
            if ends is not None:
                low_live = one_if(me) * one_if(counts_s[0, dn] - (GROUPS_DEV - 1))
                high_live = one_if(N_SEQ - 1 - me) * one_if(counts_s[0, up])
                beyond = panel[128:136].astype(BF16).astype(F32)
                put_q(nb, 4, beyond[0:4] * low_live)
                put_q(nb, 520, beyond[4:8] * high_live)
            if nb < len(beside):
                four_groups(beside[nb])

    for i in (2, 3, 4, 5):
        four_groups(i)

    for load in loads[2:5]:
        load.wait()

    def set_amount(j, carry):
        slot = slot_s[0, me * GROUPS_DEV + j]
        weight = (1 + 255 * jnp.minimum(slot, 1)) * (1 + 255 * jnp.clip(slot - 1, 0, 1)) * (
            1 + 255 * jnp.clip(slot - 2, 0, 1))
        amount_s[j] = j * weight
        return carry

    lax.fori_loop(0, GROUPS_DEV, set_amount, 0)

    def set_inv(d, carry):
        held = jnp.int32(0)
        for j in range(GROUPS_DEV):
            away = jnp.abs(owner_s[0, me * GROUPS_DEV + j] - d)
            held = held + amount_s[j] * (1 - jnp.minimum(away, 1))
        for slot in range(CAP):
            inv_s[d * CAP + slot] = jnp.minimum((held // 256 ** slot) % 256, GROUPS_DEV - 1)
        return carry

    lax.fori_loop(0, N_SEQ, set_inv, 0)
    my_count = counts_s[0, me]
    loads[5].wait()
    for load in loads[6:]:
        load.start()
    project(8, (0, 1))
    project(16, (6, 7))

    for h in halos:
        h.wait_recv()
    low = jnp.concatenate(
        [halo[0].astype(F32) * one_if(me), tok[1:4].reshape(48, C).astype(F32)], axis=0)
    high = jnp.concatenate(
        [tok[62:65].reshape(48, C).astype(F32), halo[1].astype(F32) * one_if(N_SEQ - 1 - me)], axis=0)
    for b in range(6):
        act_s[0, b, 0:40, :] = act_of(low, 40, b)
        act_s[1, b, 0:40, :] = act_of(high[8:64], 40, b)
    pairs[0] = paired(0, 16, 8)
    pairs[GROUPS_DEV - 1] = paired(1, 16, 0)
    zero = jnp.zeros((8, C2), BF16)
    ends = jnp.concatenate([paired(0, 4, 0), paired(1, 4, 32), zero], axis=0)

    relays = {}
    for kx, kz in ORDER:
        dest, k = seq_at(kx, kz), kx * 2 + kz
        for slot in range(CAP):
            group = inv_s[dest * CAP + slot]
            outgoing[dest * CAP + slot] = (pairs[group].astype(F32) * one_if(my_count - group)).astype(BF16)
        relays[k] = pltpu.make_async_remote_copy(
            outgoing.at[pl.ds(dest * CAP, CAP)], arrived.at[k - 1], a_send.at[k - 1], a_recv.at[k - 1],
            device_id=(dp, dest), device_id_type=MESH)
        relays[k].start()

    def settle(offsets):
        rows = []
        for kx, kz in offsets:
            relays[kx * 2 + kz].wait_recv()
            rows.append(arrived[kx * 2 + kz - 1].reshape(CAP * HALF, C2))
        rows = jnp.concatenate(rows, axis=0)
        for nb in range(3):
            cols = pl.ds(nb * 512, 512)
            panel = gelu(jnp.dot(rows, down[:, cols], preferred_element_type=F32)).astype(BF16)
            for n, (kx, kz) in enumerate(offsets):
                source = ((mx + 4 - kx) % 4) * 2 + (mz + 2 - kz) % 2
                owned_ref[0, pl.ds(source * CAP, CAP), :, cols] = panel[n * 64:n * 64 + 64].reshape(CAP, HALF, 512)

    project(0, ())
    project(24, (), ends)

    for slot in range(CAP):
        owned_ref[0, me * CAP + slot] = panels[inv_s[me * CAP + slot]]

    loads[6].wait()
    loads[7].wait()
    loads[8].wait()

    def mix(r):
        base = r * 128
        for cb in range(6):
            cols = pl.ds(cb * 256, 256)
            value = jnp.concatenate([
                sum(bdw[tap:tap + 1, b * 128:b * 128 + 128] * qf[b, base + 7 + tap:base + 135 + tap, :]
                    for tap in range(3))
                for b in (2 * cb, 2 * cb + 1)], axis=1)
            value = value.astype(BF16)
            mixed[base:base + 128, cols] = value
            mixed_t[pl.ds(cb * 256, 256), base:base + 128] = value.T

    def remote(src, dst, send_sem, recv_sem, device):
        return pltpu.make_async_remote_copy(
            src, dst, send_sem, recv_sem, device_id=device, device_id_type=MESH)

    def copy_core(c):
        return remote(csend.at[c], crecv.at[c], c_send.at[c], c_recv.at[c], (dp_of(my, zh, 1 - core), me))

    def make_term(c):
        cols = pl.ds(c * CW, CW)
        delta = []
        for r in range(4):
            if c == 0:
                mix(r)
            rows = pl.ds(r * 128, 128)
            pre = jnp.dot(mixed[rows, :], bott[:, cols], preferred_element_type=F32)
            value, slope = gelu_both(pre)
            out_ref[0, rows, cols] = value.astype(BF16)
            delta.append((cot[rows, cols].astype(F32) * slope).astype(BF16))
        delta = jnp.concatenate(delta, axis=0)
        for i in range(4):
            part = jnp.dot(mixed_t[pl.ds(i * 384, 384), :], delta, preferred_element_type=F32)
            gbuf[c, pl.ds(i * 4, 4)] = part.reshape(4, 2, 48, CW)
        csend[c] = gbuf[c, :, 1 - core].astype(BF16)
        copy_core(c).start()

    def core_sum(start, width, blocks, count):
        c, lanes = start // CW, pl.ds(start % CW, width)
        rows = pl.ds(blocks, count)
        return gbuf[c, rows, core, :, lanes] + crecv[c, rows, :, lanes].astype(F32)

    class Chunk:
        def __init__(self, n):
            self.start, self.width, self.direct = CHUNKS[n]
            (self.bown, self.ysend, self.yrecv, self.xacc, self.xsend, self.xrecv,
             self.zown, self.zsend, self.zrecv) = chunk_bufs[n]
            self.sems = chunk_sems[n]

        def copy_y(self, n):
            if self.direct:
                src, dst = self.ysend.at[pl.ds(2 * n, 2)], self.yrecv.at[pl.ds(2 * n, 2)]
                to = (my + n + 1) % 4
            else:
                src, dst = self.ysend.at[n], self.yrecv.at[n]
                to = (my + (1 if n < 3 else 3)) % 4
            return remote(src, dst, self.sems[0].at[n], self.sems[1].at[n], (dp_of(to, zh, core), me))

        def copy_x(self, k):
            return remote(self.xsend.at[k - 1], self.xrecv.at[k - 1], self.sems[2].at[k - 1], self.sems[3].at[k - 1],
                          (dp, seq_at(k, 0)))

        def copy_z(self, k):
            to = (dp_of(my, (zh + k // 2) % 4, core), mx * 2 + (mz + k % 2) % 2)
            return remote(self.zsend.at[k], self.zrecv.at[k - 1], self.sems[4].at[k - 1], self.sems[5].at[k - 1], to)

        def begin(self):
            def summed(y, half):
                return core_sum(self.start, self.width, y * 4 + half * 2, 2)

            if self.direct:
                for n in (1, 0, 2):
                    for half in (0, 1):
                        self.ysend[2 * n + half] = summed((my + n + 1) % 4, half).astype(BF16)
                    self.copy_y(n).start()
                self.bown[2] = summed(my, 0)
                self.bown[3] = summed(my, 1)
                return
            nxt, across, prv = (my + 1) % 4, (my + 2) % 4, (my + 3) % 4
            for n, block, half in ((0, across, 0), (3, across, 1), (1, nxt, 1), (4, prv, 0)):
                self.ysend[n] = summed(block, half).astype(BF16)
                self.copy_y(n).start()
            self.bown[0] = summed(nxt, 0)
            self.bown[1] = summed(prv, 1)
            self.bown[2] = summed(my, 0)
            self.bown[3] = summed(my, 1)

        def pass_y(self):
            if self.direct:
                return
            self.copy_y(0).wait_recv()
            self.ysend[2] = (self.bown[0] + self.yrecv[0].astype(F32)).astype(BF16)
            self.copy_y(2).start()
            self.copy_y(3).wait_recv()
            self.ysend[5] = (self.bown[1] + self.yrecv[3].astype(F32)).astype(BF16)
            self.copy_y(5).start()

        def after_y(self):
            if self.direct:
                for n in range(3):
                    self.copy_y(n).wait_recv()
                slots = (0, 2, 4), (1, 3, 5)
            else:
                for n in (1, 4, 2, 5):
                    self.copy_y(n).wait_recv()
                slots = (2, 4), (1, 5)
            half0, half1 = self.bown[2], self.bown[3]
            for n in slots[0]:
                half0 = half0 + self.yrecv[n].astype(F32)
            for n in slots[1]:
                half1 = half1 + self.yrecv[n].astype(F32)
            for h in range(2):
                self.xacc[h] = half0[h].reshape(4, 12, self.width)
                self.xacc[2 + h] = half1[h].reshape(4, 12, self.width)
            for k in (2, 1, 3):
                part = self.xacc[:, (mx + k) % 4]
                self.xsend[k - 1] = part.reshape(48, self.width).astype(BF16)
                self.copy_x(k).start()

        def after_x(self):
            total = self.xacc[:, mx].reshape(48, self.width)
            for k in range(1, 4):
                self.copy_x(k).wait_recv()
                total = total + self.xrecv[k - 1].astype(F32)
            for z in range(8):
                k = ((z // 2 + 4 - zh) % 4) * 2 + (z % 2 + 2 - mz) % 2
                part = pack8(total[z * 6:z * 6 + 6])
                self.zown[k] = part
                self.zsend[k] = part.astype(BF16)
            for k in (4, 5, 3, 7, 2, 6, 1):
                self.copy_z(k).start()

        def after_z(self):
            total = self.zown[0]
            for k in range(1, 8):
                self.copy_z(k).wait_recv()
                total = total + self.zrecv[k - 1].astype(F32)
            grad_ref[:, self.start:self.start + self.width] = unpack8(total, self.width)

        def finish(self):
            for n in range(3 if self.direct else 6):
                self.copy_y(n).wait_send()
            for k in range(1, 4):
                self.copy_x(k).wait_send()
            for k in range(1, 8):
                self.copy_z(k).wait_send()

    chunks = [Chunk(n) for n in range(len(CHUNKS))]
    early, middle, late = ([x for x in chunks if x.start // CW == c] for c in range(NC))

    def each(part, step):
        for x in part:
            getattr(x, step)()

    make_term(0)
    make_term(1)
    copy_core(0).wait_recv()
    each(early, "begin")
    make_term(2)
    copy_core(1).wait_recv()
    each(middle, "begin")
    each(early, "pass_y")
    copy_core(2).wait_recv()
    each(late, "begin")
    each(middle, "pass_y")
    each(early, "after_y")
    each(late, "pass_y")
    each(middle, "after_y")
    each(early, "after_x")
    each(late, "after_y")
    settle(ORDER[0:2])
    each(middle, "after_x")
    settle(ORDER[2:4])
    each(late, "after_x")
    settle(ORDER[4:7])
    each(chunks, "after_z")

    for k in range(1, 8):
        relays[k].wait_send()
    for h in halos:
        h.wait_send()
    for c in range(NC):
        copy_core(c).wait_send()
    each(chunks, "finish")


CHUNKS = ((0, 256, False), (256, 256, False), (512, 256, False))


def chunk_buffers(width):
    V = pltpu.VMEM
    return (
        V((4, 2, 48, width), F32), V((6, 2, 48, width), BF16), V((6, 2, 48, width), BF16),
        V((4, 4, 12, width), F32), V((3, 48, width), BF16), V((3, 48, width), BF16),
        V((8, 16, 128), F32), V((8, 16, 128), BF16), V((7, 16, 128), BF16),
    )


OUTS = (
    jax.ShapeDtypeStruct((1, GROUPS_DEV, HALF, C2), BF16),
    jax.ShapeDtypeStruct((1, HROWS, C), BF16),
    jax.ShapeDtypeStruct((6, C), F32),
)
FAR = pl.BlockSpec(memory_space=pl.ANY)


def hand_over(owned_ref, out_ref, grad_ref, owned_to, out_to, grad_to, sems):
    copies = [pltpu.make_async_copy(grad_ref, grad_to, sems.at[0])]
    for i in range(4):
        rows = pl.ds(i * 8, 8)
        copies.append(pltpu.make_async_copy(owned_ref.at[0, rows], owned_to.at[0, rows], sems.at[1 + i]))
    for i in range(2):
        rows = pl.ds(i * 256, 256)
        copies.append(pltpu.make_async_copy(out_ref.at[0, rows], out_to.at[0, rows], sems.at[5 + i]))
    for copy in copies:
        copy.start()
    for copy in copies:
        copy.wait()


def on_device(tokens, depthwise_weight, down_weight, bott_dw, bott_weight, cotangent,
              plan_owner, plan_slot, counts):
    V, S, DMA = pltpu.VMEM, pltpu.SMEM, pltpu.SemaphoreType.DMA
    made = pl.pallas_call(
        kernel,
        out_shape=tuple(pltpu.VMEM(o.shape, o.dtype) for o in OUTS),
        in_specs=[FAR] * 9,
        out_specs=(pl.BlockSpec(memory_space=pltpu.VMEM),) * 3,
        scratch_shapes=[
            S((1, 256), jnp.int32),
            S((1, 256), jnp.int32),
            S((1, 8), jnp.int32),
            S((GROUPS_DEV,), jnp.int32),
            S((GROUPS_DEV,), jnp.int32),
            V((3, C), F32),
            V((3, C2), F32),
            V((ROWS // PAD + 2, PAD, C), BF16),
            V((2, PAD, C), BF16),
            V((C2, C2), BF16),
            V((C2, C), BF16),
            V((HROWS, C), BF16),
            V((2, 6, 128, 128), F32),
            V((GROUPS_DEV, HALF, C2), BF16),
            V((GROUPS_DEV, HALF, C2), BF16),
            V((GROUPS_DEV, HALF, C2), BF16),
            V((7, CAP, HALF, C2), BF16),
            V((12, HROWS + 16, 128), F32),
            V((HROWS, C2), BF16),
            V((C2, HROWS), BF16),
            V((NC, 16, 2, 48, CW), F32),
            V((NC, 16, 48, CW), BF16),
            V((NC, 16, 48, CW), BF16),
            tuple(chunk_buffers(width) for _, width, _ in CHUNKS),
            DMA((9,)), DMA((2,)), DMA((2,)), DMA((7,)), DMA((7,)),
            DMA((NC,)), DMA((NC,)),
            tuple((DMA((6,)), DMA((6,)), DMA((3,)), DMA((3,)), DMA((7,)), DMA((7,))) for _ in CHUNKS),
        ],
        compiler_params=pltpu.CompilerParams(
            collective_id=0, has_side_effects=True, vmem_limit_bytes=56 * 1024 * 1024),
        cost_estimate=pl.CostEstimate(
            flops=5_000_000_000, bytes_accessed=14_000_000, transcendentals=2_000_000),
    )(plan_owner, plan_slot, counts, tokens.reshape(ROWS // PAD, PAD, C), depthwise_weight, down_weight,
      bott_dw, bott_weight, cotangent)
    return pl.pallas_call(
        hand_over,
        out_shape=OUTS,
        in_specs=[FAR] * 3,
        out_specs=(FAR,) * 3,
        scratch_shapes=[DMA((7,))],
        compiler_params=pltpu.CompilerParams(vmem_limit_bytes=40 * 1024 * 1024),
    )(*made)


def solution(mesh):
    placed = (
        P("dp", "seq", None),
        P(),
        P(),
        P(),
        P(),
        P("dp", "seq", None),
        P("dp", None),
        P("dp", None),
        P("dp", None),
    )
    return jax.shard_map(
        on_device,
        mesh=mesh,
        in_specs=placed,
        out_specs=(P("dp", "seq", None, None), P("dp", "seq", None), P(("dp", "seq"), None)),
        check_vma=False,
    )
```

```python
import jax
import jax.numpy as jnp
from jax import lax
from jax.experimental import pallas as pl
from jax.experimental.pallas import tpu as pltpu
from jax.sharding import PartitionSpec as P

C = 768
C2 = 1536
GROUP = 32
GROUPS_DEV = 32
HALF = 16
CAP = 4
N_SEQ = 8
ROWS = 1024
HROWS = 512
PAD = 16
NC = 3
CW = C // NC
MESH = pl.DeviceIdType.MESH
K0 = 0.7978845608028654
K1 = 0.044715
ORDER = ((2, 1), (1, 1), (3, 1), (0, 1), (2, 0), (1, 0), (3, 0))
BF16, F32 = jnp.bfloat16, jnp.float32


def gelu(x):
    half = 0.5 * x
    return half + half * jnp.tanh(x * (K0 + (K0 * K1) * (x * x)))


def gelu_both(x):
    square = x * x
    t = jnp.tanh(x * (K0 + (K0 * K1) * square))
    half = 0.5 + 0.5 * t
    slope = half + 0.5 * x * (1.0 - t * t) * (K0 + (3.0 * K0 * K1) * square)
    return x * half, slope


def one_if(n):
    return jnp.clip(n, 0, 1).astype(F32)


def pack8(v):
    v = jnp.concatenate([v, jnp.zeros((2, v.shape[1]), F32)], axis=0)
    if v.shape[1] == 128:
        return jnp.concatenate([v, jnp.zeros((8, 128), F32)], axis=0)
    return jnp.concatenate([v[:, 0:128], v[:, 128:256]], axis=0)


def unpack8(v, width):
    if width == 128:
        return v[0:6]
    return jnp.concatenate([v[0:6], v[8:14]], axis=1)


def kernel(
    owner_ref, slot_ref, counts_ref, tokens_ref, dw_ref, down_ref, bdw_ref, bott_ref, cot_ref,
    owned_ref, out_ref, grad_ref,
    owner_s, slot_s, counts_s, amount_s, inv_s, dw, bdw,
    tok, halo, down, bott, cot, act_s, pairs, panels, outgoing, arrived, qf, mixed, mixed_t,
    gbuf, csend, crecv, chunk_bufs,
    in_sem, halo_send, halo_recv, a_send, a_recv,
    c_send, c_recv, chunk_sems,
):
    dp = lax.axis_index("dp")
    me = lax.axis_index("seq")
    mx, mz = me // 2, me % 2
    core = dp % 2
    zh = (dp // 2) % 4
    my = dp // 8

    def seq_at(kx, kz):
        return ((mx + kx) % 4) * 2 + (mz + kz) % 2

    def dp_of(y, z, c):
        return y * 8 + z * 2 + c

    loads = [
        pltpu.make_async_copy(src, dst, in_sem.at[i])
        for i, (src, dst) in enumerate((
            (tokens_ref, tok.at[pl.ds(1, 64)]), (dw_ref, dw), (owner_ref, owner_s), (slot_ref, slot_s),
            (counts_ref, counts_s), (down_ref, down), (bdw_ref, bdw), (bott_ref, bott), (cot_ref.at[0], cot),
        ))
    ]
    for load in loads[0:6]:
        load.start()
    barrier = pltpu.get_barrier_semaphore()
    peers = [(dp, seq_at(k // 2, k % 2)) for k in range(1, 8)]
    peers += [(dp_of(my, zh, 1 - core), me)]
    peers += [(dp_of((my + k) % 4, zh, core), me) for k in range(1, 4)]
    peers += [(dp_of(my, (zh + k) % 4, core), mx * 2 + z) for k in range(1, 4) for z in range(2)]
    for peer in peers:
        pl.semaphore_signal(barrier, inc=1, device_id=peer, device_id_type=MESH)

    tok[0] = jnp.zeros((PAD, C), BF16)
    tok[65] = jnp.zeros((PAD, C), BF16)
    pl.semaphore_wait(barrier, len(peers))

    up, dn = (me + 1) % N_SEQ, (me + N_SEQ - 1) % N_SEQ
    halos = [
        pltpu.make_async_remote_copy(
            tokens_ref.at[63], halo.at[0],
            halo_send.at[0], halo_recv.at[0], device_id=(dp, up), device_id_type=MESH),
        pltpu.make_async_remote_copy(
            tokens_ref.at[0], halo.at[1],
            halo_send.at[1], halo_recv.at[1], device_id=(dp, dn), device_id_type=MESH),
    ]
    for h in halos:
        h.start()

    loads[0].wait()
    loads[1].wait()

    def act_of(rows, count, b):
        cols = slice(b * 128, b * 128 + 128)
        here = rows[8:8 + count, cols]
        conv = (dw[0:1, cols] * rows[0:count, cols] + dw[1:2, cols] * here
                + dw[2:3, cols] * rows[16:16 + count, cols])
        return here + gelu(conv)

    def paired(at, count, first):
        return jnp.concatenate(
            [act_s[at, b, pl.ds(first + odd, count, stride=2), :] for odd in (0, 1) for b in range(6)],
            axis=1).astype(BF16)

    def four_groups(i):
        at = i % 2
        rows = tok[8 * i:8 * i + 10].reshape(160, C).astype(F32)[8:152]
        for b in range(6):
            act_s[at, b, 0:128, :] = act_of(rows, 128, b)
        pairs[4 * i:4 * i + 4] = paired(at, 64, 0).reshape(4, HALF, C2)


    def put_q(nb, at, value):
        for b in range(4):
            qf[nb * 4 + b, at:at + value.shape[0], :] = value[:, b * 128:b * 128 + 128]

    def project(first, beside, ends=None):
        rows = pairs[first:first + 8].reshape(128, C2)
        if ends is not None:
            rows = jnp.concatenate([rows, ends], axis=0)
        for nb in range(3):
            cols = pl.ds(nb * 512, 512)
            panel = gelu(jnp.dot(rows, down[:, cols], preferred_element_type=F32))
            for n in range(8):
                value = (panel[n * HALF:n * HALF + HALF] * one_if(my_count - (first + n))).astype(BF16)
                panels[first + n, :, cols] = value
                put_q(nb, 8 + (first + n) * HALF, value.astype(F32))
            if ends is not None:
                low_live = one_if(me) * one_if(counts_s[0, dn] - (GROUPS_DEV - 1))
                high_live = one_if(N_SEQ - 1 - me) * one_if(counts_s[0, up])
                beyond = panel[128:136].astype(BF16).astype(F32)
                put_q(nb, 4, beyond[0:4] * low_live)
                put_q(nb, 520, beyond[4:8] * high_live)
            if nb < len(beside):
                four_groups(beside[nb])

    for i in (2, 3, 4, 5):
        four_groups(i)

    for load in loads[2:5]:
        load.wait()

    def set_amount(j, carry):
        slot = slot_s[0, me * GROUPS_DEV + j]
        weight = (1 + 255 * jnp.minimum(slot, 1)) * (1 + 255 * jnp.clip(slot - 1, 0, 1)) * (
            1 + 255 * jnp.clip(slot - 2, 0, 1))
        amount_s[j] = j * weight
        return carry

    lax.fori_loop(0, GROUPS_DEV, set_amount, 0)

    def set_inv(d, carry):
        held = jnp.int32(0)
        for j in range(GROUPS_DEV):
            away = jnp.abs(owner_s[0, me * GROUPS_DEV + j] - d)
            held = held + amount_s[j] * (1 - jnp.minimum(away, 1))
        for slot in range(CAP):
            inv_s[d * CAP + slot] = jnp.minimum((held // 256 ** slot) % 256, GROUPS_DEV - 1)
        return carry

    lax.fori_loop(0, N_SEQ, set_inv, 0)
    my_count = counts_s[0, me]
    loads[5].wait()
    for load in loads[6:]:
        load.start()
    project(8, (0, 1))
    project(16, (6, 7))

    for h in halos:
        h.wait_recv()
    low = jnp.concatenate(
        [halo[0].astype(F32) * one_if(me), tok[1:4].reshape(48, C).astype(F32)], axis=0)
    high = jnp.concatenate(
        [tok[62:65].reshape(48, C).astype(F32), halo[1].astype(F32) * one_if(N_SEQ - 1 - me)], axis=0)
    for b in range(6):
        act_s[0, b, 0:40, :] = act_of(low, 40, b)
        act_s[1, b, 0:40, :] = act_of(high[8:64], 40, b)
    pairs[0] = paired(0, 16, 8)
    pairs[GROUPS_DEV - 1] = paired(1, 16, 0)
    zero = jnp.zeros((8, C2), BF16)
    ends = jnp.concatenate([paired(0, 4, 0), paired(1, 4, 32), zero], axis=0)

    relays = {}
    for kx, kz in ORDER:
        dest, k = seq_at(kx, kz), kx * 2 + kz
        for slot in range(CAP):
            group = inv_s[dest * CAP + slot]
            outgoing[dest * CAP + slot] = (pairs[group].astype(F32) * one_if(my_count - group)).astype(BF16)
        relays[k] = pltpu.make_async_remote_copy(
            outgoing.at[pl.ds(dest * CAP, CAP)], arrived.at[k - 1], a_send.at[k - 1], a_recv.at[k - 1],
            device_id=(dp, dest), device_id_type=MESH)
        relays[k].start()

    def settle(offsets):
        rows = []
        for kx, kz in offsets:
            relays[kx * 2 + kz].wait_recv()
            rows.append(arrived[kx * 2 + kz - 1].reshape(CAP * HALF, C2))
        rows = jnp.concatenate(rows, axis=0)
        for nb in range(3):
            cols = pl.ds(nb * 512, 512)
            panel = gelu(jnp.dot(rows, down[:, cols], preferred_element_type=F32)).astype(BF16)
            for n, (kx, kz) in enumerate(offsets):
                source = ((mx + 4 - kx) % 4) * 2 + (mz + 2 - kz) % 2
                owned_ref[0, pl.ds(source * CAP, CAP), :, cols] = panel[n * 64:n * 64 + 64].reshape(CAP, HALF, 512)

    project(0, ())
    project(24, (), ends)

    for slot in range(CAP):
        owned_ref[0, me * CAP + slot] = panels[inv_s[me * CAP + slot]]

    loads[6].wait()
    loads[7].wait()
    loads[8].wait()

    def mix(r):
        base = r * 128
        for cb in range(6):
            cols = pl.ds(cb * 256, 256)
            value = jnp.concatenate([
                sum(bdw[tap:tap + 1, b * 128:b * 128 + 128] * qf[b, base + 7 + tap:base + 135 + tap, :]
                    for tap in range(3))
                for b in (2 * cb, 2 * cb + 1)], axis=1)
            value = value.astype(BF16)
            mixed[base:base + 128, cols] = value
            mixed_t[pl.ds(cb * 256, 256), base:base + 128] = value.T

    def remote(src, dst, send_sem, recv_sem, device):
        return pltpu.make_async_remote_copy(
            src, dst, send_sem, recv_sem, device_id=device, device_id_type=MESH)

    def copy_core(c):
        return remote(csend.at[c], crecv.at[c], c_send.at[c], c_recv.at[c], (dp_of(my, zh, 1 - core), me))

    def make_term(c):
        cols = pl.ds(c * CW, CW)
        delta = []
        for r in range(4):
            if c == 0:
                mix(r)
            rows = pl.ds(r * 128, 128)
            pre = jnp.dot(mixed[rows, :], bott[:, cols], preferred_element_type=F32)
            value, slope = gelu_both(pre)
            out_ref[0, rows, cols] = value.astype(BF16)
            delta.append((cot[rows, cols].astype(F32) * slope).astype(BF16))
        delta = jnp.concatenate(delta, axis=0)
        for i in range(4):
            part = jnp.dot(mixed_t[pl.ds(i * 384, 384), :], delta, preferred_element_type=F32)
            gbuf[c, pl.ds(i * 4, 4)] = part.reshape(4, 2, 48, CW)
        csend[c] = gbuf[c, :, 1 - core].astype(BF16)
        copy_core(c).start()

    def core_sum(start, width, blocks, count):
        c, lanes = start // CW, pl.ds(start % CW, width)
        rows = pl.ds(blocks, count)
        return gbuf[c, rows, core, :, lanes] + crecv[c, rows, :, lanes].astype(F32)

    class Chunk:
        def __init__(self, n):
            self.start, self.width, self.direct = CHUNKS[n]
            (self.bown, self.ysend, self.yrecv, self.xacc, self.xsend, self.xrecv,
             self.zown, self.zsend, self.zrecv) = chunk_bufs[n]
            self.sems = chunk_sems[n]

        def copy_y(self, n):
            if self.direct:
                src, dst = self.ysend.at[pl.ds(2 * n, 2)], self.yrecv.at[pl.ds(2 * n, 2)]
                to = (my + n + 1) % 4
            else:
                src, dst = self.ysend.at[n], self.yrecv.at[n]
                to = (my + (1 if n < 3 else 3)) % 4
            return remote(src, dst, self.sems[0].at[n], self.sems[1].at[n], (dp_of(to, zh, core), me))

        def copy_x(self, k):
            return remote(self.xsend.at[k - 1], self.xrecv.at[k - 1], self.sems[2].at[k - 1], self.sems[3].at[k - 1],
                          (dp, seq_at(k, 0)))

        def copy_z(self, k):
            to = (dp_of(my, (zh + k // 2) % 4, core), mx * 2 + (mz + k % 2) % 2)
            return remote(self.zsend.at[k], self.zrecv.at[k - 1], self.sems[4].at[k - 1], self.sems[5].at[k - 1], to)

        def begin(self):
            def summed(y, half):
                return core_sum(self.start, self.width, y * 4 + half * 2, 2)

            if self.direct:
                for n in (1, 0, 2):
                    for half in (0, 1):
                        self.ysend[2 * n + half] = summed((my + n + 1) % 4, half).astype(BF16)
                    self.copy_y(n).start()
                self.bown[2] = summed(my, 0)
                self.bown[3] = summed(my, 1)
                return
            nxt, across, prv = (my + 1) % 4, (my + 2) % 4, (my + 3) % 4
            for n, block, half in ((0, across, 0), (3, across, 1), (1, nxt, 1), (4, prv, 0)):
                self.ysend[n] = summed(block, half).astype(BF16)
                self.copy_y(n).start()
            self.bown[0] = summed(nxt, 0)
            self.bown[1] = summed(prv, 1)
            self.bown[2] = summed(my, 0)
            self.bown[3] = summed(my, 1)

        def pass_y(self):
            if self.direct:
                return
            self.copy_y(0).wait_recv()
            self.ysend[2] = (self.bown[0] + self.yrecv[0].astype(F32)).astype(BF16)
            self.copy_y(2).start()
            self.copy_y(3).wait_recv()
            self.ysend[5] = (self.bown[1] + self.yrecv[3].astype(F32)).astype(BF16)
            self.copy_y(5).start()

        def after_y(self):
            if self.direct:
                for n in range(3):
                    self.copy_y(n).wait_recv()
                slots = (0, 2, 4), (1, 3, 5)
            else:
                for n in (1, 4, 2, 5):
                    self.copy_y(n).wait_recv()
                slots = (2, 4), (1, 5)
            half0, half1 = self.bown[2], self.bown[3]
            for n in slots[0]:
                half0 = half0 + self.yrecv[n].astype(F32)
            for n in slots[1]:
                half1 = half1 + self.yrecv[n].astype(F32)
            for h in range(2):
                self.xacc[h] = half0[h].reshape(4, 12, self.width)
                self.xacc[2 + h] = half1[h].reshape(4, 12, self.width)
            for k in (2, 1, 3):
                part = self.xacc[:, (mx + k) % 4]
                self.xsend[k - 1] = part.reshape(48, self.width).astype(BF16)
                self.copy_x(k).start()

        def after_x(self):
            total = self.xacc[:, mx].reshape(48, self.width)
            for k in range(1, 4):
                self.copy_x(k).wait_recv()
                total = total + self.xrecv[k - 1].astype(F32)
            for z in range(8):
                k = ((z // 2 + 4 - zh) % 4) * 2 + (z % 2 + 2 - mz) % 2
                part = pack8(total[z * 6:z * 6 + 6])
                self.zown[k] = part
                self.zsend[k] = part.astype(BF16)
            for k in (4, 5, 3, 7, 2, 6, 1):
                self.copy_z(k).start()

        def after_z(self):
            total = self.zown[0]
            for k in range(1, 8):
                self.copy_z(k).wait_recv()
                total = total + self.zrecv[k - 1].astype(F32)
            grad_ref[:, self.start:self.start + self.width] = unpack8(total, self.width)

        def finish(self):
            for n in range(3 if self.direct else 6):
                self.copy_y(n).wait_send()
            for k in range(1, 4):
                self.copy_x(k).wait_send()
            for k in range(1, 8):
                self.copy_z(k).wait_send()

    chunks = [Chunk(n) for n in range(len(CHUNKS))]
    early, middle, late = ([x for x in chunks if x.start // CW == c] for c in range(NC))

    def each(part, step):
        for x in part:
            getattr(x, step)()

    make_term(0)
    make_term(1)
    copy_core(0).wait_recv()
    each(early, "begin")
    make_term(2)
    copy_core(1).wait_recv()
    each(middle, "begin")
    each(early, "pass_y")
    copy_core(2).wait_recv()
    each(late, "begin")
    each(middle, "pass_y")
    each(early, "after_y")
    each(late, "pass_y")
    each(middle, "after_y")
    each(early, "after_x")
    each(late, "after_y")
    settle(ORDER[0:2])
    each(middle, "after_x")
    settle(ORDER[2:4])
    each(late, "after_x")
    settle(ORDER[4:7])
    each(chunks, "after_z")

    for k in range(1, 8):
        relays[k].wait_send()
    for h in halos:
        h.wait_send()
    for c in range(NC):
        copy_core(c).wait_send()
    each(chunks, "finish")


CHUNKS = ((0, 256, False), (256, 256, False), (512, 256, True))


def chunk_buffers(width):
    V = pltpu.VMEM
    return (
        V((4, 2, 48, width), F32), V((6, 2, 48, width), BF16), V((6, 2, 48, width), BF16),
        V((4, 4, 12, width), F32), V((3, 48, width), BF16), V((3, 48, width), BF16),
        V((8, 16, 128), F32), V((8, 16, 128), BF16), V((7, 16, 128), BF16),
    )


OUTS = (
    jax.ShapeDtypeStruct((1, GROUPS_DEV, HALF, C2), BF16),
    jax.ShapeDtypeStruct((1, HROWS, C), BF16),
    jax.ShapeDtypeStruct((6, C), F32),
)
FAR = pl.BlockSpec(memory_space=pl.ANY)


def hand_over(owned_ref, out_ref, grad_ref, owned_to, out_to, grad_to, sems):
    copies = [pltpu.make_async_copy(grad_ref, grad_to, sems.at[0])]
    for i in range(4):
        rows = pl.ds(i * 8, 8)
        copies.append(pltpu.make_async_copy(owned_ref.at[0, rows], owned_to.at[0, rows], sems.at[1 + i]))
    for i in range(2):
        rows = pl.ds(i * 256, 256)
        copies.append(pltpu.make_async_copy(out_ref.at[0, rows], out_to.at[0, rows], sems.at[5 + i]))
    for copy in copies:
        copy.start()
    for copy in copies:
        copy.wait()


def on_device(tokens, depthwise_weight, down_weight, bott_dw, bott_weight, cotangent,
              plan_owner, plan_slot, counts):
    V, S, DMA = pltpu.VMEM, pltpu.SMEM, pltpu.SemaphoreType.DMA
    made = pl.pallas_call(
        kernel,
        out_shape=tuple(pltpu.VMEM(o.shape, o.dtype) for o in OUTS),
        in_specs=[FAR] * 9,
        out_specs=(pl.BlockSpec(memory_space=pltpu.VMEM),) * 3,
        scratch_shapes=[
            S((1, 256), jnp.int32),
            S((1, 256), jnp.int32),
            S((1, 8), jnp.int32),
            S((GROUPS_DEV,), jnp.int32),
            S((GROUPS_DEV,), jnp.int32),
            V((3, C), F32),
            V((3, C2), F32),
            V((ROWS // PAD + 2, PAD, C), BF16),
            V((2, PAD, C), BF16),
            V((C2, C2), BF16),
            V((C2, C), BF16),
            V((HROWS, C), BF16),
            V((2, 6, 128, 128), F32),
            V((GROUPS_DEV, HALF, C2), BF16),
            V((GROUPS_DEV, HALF, C2), BF16),
            V((GROUPS_DEV, HALF, C2), BF16),
            V((7, CAP, HALF, C2), BF16),
            V((12, HROWS + 16, 128), F32),
            V((HROWS, C2), BF16),
            V((C2, HROWS), BF16),
            V((NC, 16, 2, 48, CW), F32),
            V((NC, 16, 48, CW), BF16),
            V((NC, 16, 48, CW), BF16),
            tuple(chunk_buffers(width) for _, width, _ in CHUNKS),
            DMA((9,)), DMA((2,)), DMA((2,)), DMA((7,)), DMA((7,)),
            DMA((NC,)), DMA((NC,)),
            tuple((DMA((6,)), DMA((6,)), DMA((3,)), DMA((3,)), DMA((7,)), DMA((7,))) for _ in CHUNKS),
        ],
        compiler_params=pltpu.CompilerParams(
            collective_id=0, has_side_effects=True, vmem_limit_bytes=56 * 1024 * 1024),
        cost_estimate=pl.CostEstimate(
            flops=5_000_000_000, bytes_accessed=14_000_000, transcendentals=2_000_000),
    )(plan_owner, plan_slot, counts, tokens.reshape(ROWS // PAD, PAD, C), depthwise_weight, down_weight,
      bott_dw, bott_weight, cotangent)
    return pl.pallas_call(
        hand_over,
        out_shape=OUTS,
        in_specs=[FAR] * 3,
        out_specs=(FAR,) * 3,
        scratch_shapes=[DMA((7,))],
        compiler_params=pltpu.CompilerParams(vmem_limit_bytes=40 * 1024 * 1024),
    )(*made)


def solution(mesh):
    placed = (
        P("dp", "seq", None),
        P(),
        P(),
        P(),
        P(),
        P("dp", "seq", None),
        P("dp", None),
        P("dp", None),
        P("dp", None),
    )
    return jax.shard_map(
        on_device,
        mesh=mesh,
        in_specs=placed,
        out_specs=(P("dp", "seq", None, None), P("dp", "seq", None), P(("dp", "seq"), None)),
        check_vma=False,
    )
```
